256 devices in a mesh: section: 16 (over z_hi, x), inner: 16 (over z_lo, y, core).
Axes of the slice: x: 4, y: 4, z: 8 (z_hi: 4, z_lo: 2; z = z_hi * 2 + z_lo), core: 2. Of those that a mesh axis runs over, the one named last changes fastest.
Arguments:
- wavefunction: float32 [256, 64, 1024], P(('section', 'inner'))
- environments: bfloat16 [512, 34, 4096], P(('section', 'inner')), as said below
- mpo_terms: bfloat16 [34, 16, 16], replicated, as said below
- sector_dims: int32 [256, 2], P(('section', 'inner')), may hold values from 32 to 64, as said below
- channel_charges: int32 [34], replicated, may hold values from -1 to 1, as said below
Outputs:
- optimized: float32 [256, 64, 1024], P(('section', 'inner'))
- energy: float32 [16], P('section')
The draws below stay inside these ranges and needn't reach their ends.
Inputs may be any that keep to these rules, and one draw needn't show every extreme that they name: Each 64 x 64 matrix of environments is symmetric. Each 16 x 16 matrix of mpo_terms is symmetric. `sector_dims`: at least one block has 64 live states on both sides. `channel_charges`: both -1 and 1 occur among the channels.
All inputs are finite; a program needn't handle non-finite values.
Results may differ from the reference program's by a relative error of at most 0.02.
Values may be sent and summed in bfloat16 or wider, within the bound.
A program may use at most 128 MiB of HBM per device.

```python
import math
import jax
import jax.numpy as jnp
from jax import lax

BLK = 64
CHAN = 34
PH = 16
SEC_DEV = 1
ITERS = 2
SECT = 256
PAIR_BLOCKS = 32
PAIRS = 8
N_INNER = 16


def draw_wavefunction(key, part):
    key = jax.random.fold_in(key, 11)
    key_base, key_rows, key_cols = jax.random.split(key, 3)
    shape = (SECT, BLK, PH * BLK)
    base = jnp.clip(jax.random.normal(key_base, shape, jnp.float32), -6.0, 6.0)
    rows = jnp.exp(jax.random.uniform(key_rows, (SECT, BLK, 1), jnp.float32, 0.0, math.log(10.0))) / 3.0
    cols = jnp.exp(jax.random.uniform(key_cols, (SECT, 1, PH * BLK), jnp.float32, 0.0, math.log(10.0))) / 3.0
    position = (jnp.arange(SECT) % PAIR_BLOCKS).astype(jnp.float32)
    rising = 1.0 + 2.0 * position / max(PAIR_BLOCKS - 1, 1)
    return (base * rows * cols * rising[:, None, None]).astype(jnp.float32)


def draw_environments(key, part):
    key = jax.random.fold_in(key, 12)
    key_base, key_scale = jax.random.split(key)
    shape = (2 * SECT, CHAN, BLK, BLK)
    base = jax.random.normal(key_base, shape, jnp.float32)
    symmetric = (base + jnp.swapaxes(base, 2, 3)) * 0.5 ** 0.5
    scales = jnp.exp(jax.random.uniform(key_scale, (2 * SECT, CHAN, 1, 1), jnp.float32, math.log(0.5), math.log(2.0)))
    values = symmetric * scales / math.sqrt(BLK)
    return values.reshape(2 * SECT, CHAN, BLK * BLK).astype(jnp.bfloat16)


def draw_mpo_terms(key, part):
    key = jax.random.fold_in(key, 13)
    shape = (CHAN, PH, PH)
    base = jax.random.normal(key, shape, jnp.float32)
    symmetric = (base + jnp.swapaxes(base, 1, 2)) * 0.5 ** 0.5
    return (symmetric / math.sqrt(PH * CHAN)).astype(jnp.bfloat16)


def draw_sector_dims(key, part):
    key = jax.random.fold_in(key, 14)
    dims = jax.random.randint(key, (SECT, 2), BLK // 2, BLK + 1, jnp.int32)
    return dims.at[0].set(BLK)


def draw_channel_charges(key, part):
    key = jax.random.fold_in(key, 15)
    key_vals, key_perm = jax.random.split(key)
    charges = jax.random.randint(key_vals, (CHAN,), -1, 2, jnp.int32)
    order = jax.random.permutation(key_perm, CHAN)
    charges = charges.at[order[0]].set(-1)
    charges = charges.at[order[1]].set(1)
    return charges.astype(jnp.int32)


def setup_inputs(seed: int = 0) -> dict:
    seeds = jax.random.split(jax.random.key(seed), 6)
    return {
        "wavefunction": draw_wavefunction(jax.random.fold_in(seeds[5], 71), 0),
        "environments": draw_environments(jax.random.fold_in(seeds[5], 71), 0),
        "mpo_terms": draw_mpo_terms(jax.random.fold_in(seeds[5], 71), 0),
        "sector_dims": draw_sector_dims(jax.random.fold_in(seeds[5], 71), 0),
        "channel_charges": draw_channel_charges(jax.random.fold_in(seeds[5], 71), 0),
    }


EPSILON = 1e-06

def build_mask(dims):
    rows = jnp.arange(BLK)[None, :, None]
    cols = (jnp.arange(PH * BLK) % BLK)[None, None, :]
    live = (rows < dims[:, 0][:, None, None]) & (cols < dims[:, 1][:, None, None])
    return live.astype(jnp.float32)

def apply_operator(vector, left, right, mpo_terms, mask, channel_charges):
    lowered = lax.optimization_barrier(vector.astype(jnp.bfloat16))
    grid = lowered.reshape(2, N_INNER, SEC_DEV, BLK, PH * BLK)
    shifted = jnp.stack([jnp.roll(grid, 1, axis=1), grid, jnp.roll(grid, -1, axis=1)])
    shifted = shifted.reshape(3, PAIR_BLOCKS, BLK, PH * BLK)
    shifted = jnp.swapaxes(shifted, 0, 1)
    pick = channel_charges.astype(jnp.int32) + 1

    def one_block(items):
        triple, left_env, right_env, live = items
        source = jnp.take(triple, pick, axis=0).astype(jnp.float32)
        left_mat = left_env.astype(jnp.float32).reshape(CHAN, BLK, BLK)
        first = jnp.einsum('alm,amn->aln', left_mat, source).astype(jnp.bfloat16)
        first = lax.optimization_barrier(first).astype(jnp.float32).reshape(CHAN, BLK, PH, BLK)
        mixed = jnp.einsum('alsr,ast->altr', first, mpo_terms.astype(jnp.float32)).astype(jnp.bfloat16)
        mixed = lax.optimization_barrier(mixed).astype(jnp.float32)
        right_mat = right_env.astype(jnp.float32).reshape(CHAN, BLK, BLK)
        image = jnp.einsum('altr,aqr->ltq', mixed, right_mat)
        return image.reshape(BLK, PH * BLK) * live
    return lax.map(one_block, (shifted, left, right, mask))

def reference(wavefunction, environments, mpo_terms, sector_dims, channel_charges):
    fields = wavefunction.reshape(PAIRS, PAIR_BLOCKS, BLK, PH * BLK)
    envs = environments.reshape(PAIRS, 2, N_INNER, 2, SEC_DEV, CHAN, BLK * BLK)
    lefts = envs[:, 0].transpose(0, 2, 1, 3, 4, 5).reshape(PAIRS, PAIR_BLOCKS, CHAN, BLK * BLK)
    rights = envs[:, 1].transpose(0, 2, 1, 3, 4, 5).reshape(PAIRS, PAIR_BLOCKS, CHAN, BLK * BLK)
    dims_all = sector_dims.reshape(PAIRS, PAIR_BLOCKS, 2)
    entries = 1.0 * PAIR_BLOCKS * BLK * PH * BLK

    def boundary(items):
        field, left, right, dims = items
        mask = build_mask(dims)

        def inner_product(first_vec, second_vec):
            return jnp.sum(first_vec * second_vec) / entries
        start = field * mask
        psi = start / jnp.sqrt(inner_product(start, start) + EPSILON)
        image = apply_operator(psi, left, right, mpo_terms, mask, channel_charges)
        energy_now = inner_product(psi, image)
        lowest = energy_now
        for iteration in range(ITERS):
            resid = image - energy_now * psi
            direction = resid / jnp.sqrt(inner_product(resid, resid) + EPSILON)
            turned = apply_operator(direction, left, right, mpo_terms, mask, channel_charges)
            coupling = inner_product(direction, image)
            curvature = inner_product(direction, turned)
            angle = 0.5 * jnp.arctan2(-coupling, 0.5 * (curvature - energy_now))
            lowest = 0.5 * (energy_now + curvature) - jnp.sqrt(0.25 * (energy_now - curvature) ** 2 + coupling ** 2)
            psi = jnp.cos(angle) * psi + jnp.sin(angle) * direction
            image = jnp.cos(angle) * image + jnp.sin(angle) * turned
            energy_now = inner_product(psi, image)
        return (psi, lowest)
    psis, lows = lax.map(boundary, (fields, lefts, rights, dims_all))
    optimized = psis.reshape(SECT, BLK, PH * BLK)
    energy = jnp.repeat(lows, 2)
    return (optimized, energy)
```

```python
import functools

import jax
import jax.numpy as jnp
from jax import lax
from jax.experimental import pallas as pl
from jax.experimental.pallas import tpu as pltpu
from jax.sharding import PartitionSpec as P

MESH = pl.DeviceIdType.MESH
F32 = jnp.float32
BF16 = jnp.bfloat16

ITERS = 2
EPSILON = 1e-06
BLK = 64
CHAN = 34
PH = 16
WIDTH = PH * BLK
HALF = CHAN // 2

GROUPS = (
    tuple((0, d) for d in range(8)),
    ((0, 0), (0, 8), (1, 0), (1, 8)),
)
SLOTS = sum(len(group) for group in GROUPS)


def flipped(index, bits):
    for bit in (1, 2, 4, 8):
        if bits & bit:
            index = index + bit * (1 - 2 * ((index // bit) % 2))
    return index


def low_half(rows):
    return lax.broadcasted_iota(jnp.int32, (rows, 128), 1) < BLK


def interchange(a, b, low):
    turned_a = pltpu.roll(a, BLK, 1)
    turned_b = pltpu.roll(b, BLK, 1)
    return jnp.where(low, a, turned_b), jnp.where(low, turned_a, b)


def to_mixed(field):
    low = low_half(16)
    rows = []
    for j in range(PH // 2):
        even, odd = [], []
        for p in range(2):
            a = field[32 * p : 32 * p + 16, 128 * j : 128 * j + 128]
            b = field[32 * p + 16 : 32 * p + 32, 128 * j : 128 * j + 128]
            first, second = interchange(a, b, low)
            even.append(first)
            odd.append(second)
        rows.append(jnp.concatenate(even, axis=1))
        rows.append(jnp.concatenate(odd, axis=1))
    return rows


def kernel(
    wave_ref, env_ref, mpo_ref, dims_ref, charge_ref, psi_ref, energy_ref,
    raw, wide, lsel, rsel, wsel, first, fields, image, sources,
    halo, mask, start_buf, vec_im, vec_q, vec_t, exchange,
    env_send, env_recv, halo_send, halo_recv, red_send, red_recv,
):
    section, inner = lax.axis_index("section"), lax.axis_index("inner")
    n_inner = lax.axis_size("inner")
    parity = section % 2
    entries = 2.0 * n_inner * BLK * WIDTH

    def at(h, d):
        return (flipped(section, h), flipped(inner, d))

    above = (section, (inner + 1) % n_inner)
    below = (section, (inner + n_inner - 1) % n_inner)
    partner = at(1, 0)

    peers = [at(h, d) for group in GROUPS for h, d in group[1:]] + [above, below, partner]
    barrier = pltpu.get_barrier_semaphore()
    for peer in peers:
        pl.semaphore_signal(barrier, inc=1, device_id=peer, device_id_type=MESH)

    kept = pltpu.make_async_copy(env_ref.at[parity], raw.at[parity], env_recv.at[parity])
    kept.start()

    def dot_rows(pairs):
        rows = []
        for x, y in pairs:
            prod = x * y
            tot = None
            for i in range(BLK // 8):
                for j in range(WIDTH // 128):
                    tile = prod[8 * i : 8 * i + 8, 128 * j : 128 * j + 128]
                    tot = tile if tot is None else tot + tile
            rows.append(jnp.sum(tot, axis=0, keepdims=True))
        rows.append(jnp.zeros((8 - len(rows), 128), F32))
        return jnp.concatenate(rows, axis=0)

    def red_base(phase):
        return sum(len(group) for group in GROUPS[:phase])

    def red_start(slot, phase, value):
        base = red_base(phase)
        exchange[slot, base] = value
        for j, (h, d) in enumerate(GROUPS[phase][1:]):
            pltpu.make_async_remote_copy(
                src_ref=exchange.at[slot, base],
                dst_ref=exchange.at[slot, base + 1 + j],
                send_sem=red_send.at[slot, phase],
                recv_sem=red_recv.at[slot, phase],
                device_id=at(h, d),
                device_id_type=MESH,
            ).start()

    def red_finish(slot, phase):
        base, count = red_base(phase), len(GROUPS[phase])
        arrived = exchange.at[slot, pl.ds(base + 1, count - 1)]
        pltpu.make_async_copy(arrived, arrived, red_recv.at[slot, phase]).wait()
        parts = [exchange[slot, base + j] for j in range(count)]
        while len(parts) > 1:
            parts = [parts[2 * k] + parts[2 * k + 1] for k in range(len(parts) // 2)]
        return parts[0]

    def red_total(slot):
        value = red_finish(slot, 0)
        for phase in range(1, len(GROUPS)):
            red_start(slot, phase, value)
            value = red_finish(slot, phase)
        return jnp.sum(value, axis=1, keepdims=True) * (1.0 / entries)

    def red_drain(slot):
        for phase in range(len(GROUPS)):
            base, count = red_base(phase), len(GROUPS[phase])
            sent = exchange.at[slot, pl.ds(base + 1, count - 1)]
            pltpu.make_async_copy(sent, sent, red_send.at[slot, phase]).wait()

    def halo_copies(k):
        return [
            pltpu.make_async_remote_copy(
                src_ref=halo.at[k, 1],
                dst_ref=halo.at[k, 2 * side],
                send_sem=halo_send.at[k, side],
                recv_sem=halo_recv.at[k, side],
                device_id=target,
                device_id_type=MESH,
            )
            for side, target in ((0, above), (1, below))
        ]

    def apply():
        def left_step(c, _):
            rows = pl.ds(pl.multiple_of(c * (HALF * BLK), HALF * BLK), HALF * BLK)
            out = jnp.dot(lsel[rows, :], sources[...], preferred_element_type=F32).astype(BF16)
            for k in range(HALF):
                parts = to_mixed(out[k * BLK : (k + 1) * BLK])
                for s in range(PH):
                    first[c * HALF + k, 16 * s : 16 * s + 16, :] = parts[s]
            return 0

        lax.fori_loop(0, 2, left_step, 0)

        image[...] = jnp.zeros_like(image)

        def right_step(c, _):
            mixed = [
                jnp.dot(wsel[c * HALF + k], first[c * HALF + k], preferred_element_type=F32).astype(BF16)
                for k in range(HALF)
            ]
            right = rsel[pl.ds(c * HALF, HALF)].reshape(HALF * 256, 256)
            image[...] += jnp.dot(jnp.concatenate(mixed, axis=1), right, preferred_element_type=F32)
            return 0

        lax.fori_loop(0, 2, right_step, 0)

        low = low_half(16)
        for j in range(PH // 2):
            for p in range(2):
                a = image[32 * j : 32 * j + 16, 128 * p : 128 * p + 128]
                b = image[32 * j + 16 : 32 * j + 32, 128 * p : 128 * p + 128]
                upper, lower = interchange(a, b, low)
                lanes = slice(128 * j, 128 * j + 128)
                vec_t[32 * p : 32 * p + 16, lanes] = upper * mask[32 * p : 32 * p + 16, :]
                vec_t[32 * p + 16 : 32 * p + 32, lanes] = lower * mask[32 * p + 16 : 32 * p + 32, :]

    def scalar(total, k):
        return total[k : k + 1, :]

    row = lax.broadcasted_iota(jnp.int32, (BLK, 128), 0)
    lane = lax.broadcasted_iota(jnp.int32, (BLK, 128), 1)
    live = (row < dims_ref[0, 0]) & (lane % BLK < dims_ref[0, 1])
    mask[...] = jnp.where(live, 1.0, 0.0).astype(F32)
    start = wave_ref[0] * jnp.concatenate([mask[...]] * (WIDTH // 128), axis=1)
    start_buf[...] = start
    halo[0, 1] = start.astype(BF16)
    norm_rows = dot_rows([(start, start)])

    pl.semaphore_wait(barrier, len(peers))
    outgoing = pltpu.make_async_remote_copy(
        src_ref=env_ref.at[1 - parity],
        dst_ref=raw.at[parity],
        send_sem=env_send,
        recv_sem=env_recv.at[parity],
        device_id=partner,
        device_id_type=MESH,
    )
    outgoing.start()
    start_halo = halo_copies(0)
    for copy in start_halo:
        copy.start()
    red_start(0, 0, norm_rows)

    spread = (
        lax.broadcasted_iota(jnp.int32, (PH, 256), 1) // 16 == lax.broadcasted_iota(jnp.int32, (PH, 256), 0)
    ).astype(BF16)
    spread_rows = (
        lax.broadcasted_iota(jnp.int32, (256, PH), 0) // 16 == lax.broadcasted_iota(jnp.int32, (256, PH), 1)
    ).astype(BF16)
    same = (
        lax.broadcasted_iota(jnp.int32, (256, 256), 0) % 16 == lax.broadcasted_iota(jnp.int32, (256, 256), 1) % 16
    )

    def mpo_step(c, _):
        for k in range(HALF):
            a = c * HALF + k
            lanes = jnp.dot(mpo_ref[a], spread, preferred_element_type=F32).astype(BF16)
            both = jnp.dot(spread_rows, lanes, preferred_element_type=F32)
            wsel[a] = jnp.where(same, both, 0.0).astype(BF16)
        return 0

    lax.fori_loop(0, 2, mpo_step, 0)

    def unfold(slot):
        for j in range(BLK // 2):
            pair = raw[slot, :, 128 * j : 128 * j + 128].astype(F32)
            wide[slot, pl.ds(2 * j, CHAN, stride=BLK), :] = pair
            wide[slot, pl.ds(2 * j + 1, CHAN, stride=BLK), :] = pair

    own = (row % 2 == 0) == (lane < BLK)

    def doubled(slot, a):
        x = wide[slot, pl.ds(pl.multiple_of(a * BLK, BLK), BLK), :]
        return jnp.where(own, x, pltpu.roll(x, BLK, 1))

    kept.wait()
    unfold(parity)
    arrived = raw.at[1 - parity]
    pltpu.make_async_copy(arrived, arrived, env_recv.at[1 - parity]).wait()
    unfold(1 - parity)

    low64 = lane < BLK

    def env_step(c, _):
        for k in range(HALF):
            a = c * HALF + k
            charge = charge_ref[a]
            rows = pl.ds(pl.multiple_of(a * BLK, BLK), BLK)
            left = doubled(0, a)
            wanted = jnp.where(low64, -1, 0)
            lsel[rows, 0:128] = jnp.where(wanted == charge, left, 0.0).astype(BF16)
            lsel[rows, 128:192] = jnp.where(low64 & (charge == 1), left, 0.0).astype(BF16)[:, :BLK]
            right = doubled(1, a).astype(BF16)
            zero = jnp.zeros((2 * BLK, 128), BF16)
            block = jnp.concatenate(
                [jnp.where(low64, right, jnp.zeros_like(right)), jnp.where(low64, jnp.zeros_like(right), right)], axis=0
            )
            rsel[a, 0:128, 0:128] = block
            rsel[a, 128:256, 128:256] = block
            rsel[a, 0:128, 128:256] = zero
            rsel[a, 128:256, 0:128] = zero
        return 0

    lax.fori_loop(0, 2, env_step, 0)

    for copy in start_halo:
        copy.wait_recv()
    for k in range(3):
        sources[k * BLK : (k + 1) * BLK, :] = halo[0, k]
    norm = scalar(red_total(0), 0)
    scale = 1.0 / jnp.sqrt(norm + EPSILON)
    apply()
    im = vec_t[...] * scale
    vec_im[...] = im
    halo[1, 1] = im.astype(BF16)
    halos = [halo_copies(1), halo_copies(2)]
    for copy in halos[0]:
        copy.start()
    psi = start_buf[...] * scale
    start_buf[...] = psi
    red_start(1, 0, dot_rows([(psi, im), (im, im)]))
    totals = red_total(1)
    energy_now = scalar(totals, 0)
    unit = jnp.sqrt(scalar(totals, 1) + EPSILON)
    inverse = 1.0 / unit

    vec_q[...] = (vec_im[...] - energy_now * start_buf[...]) * inverse
    for copy in halos[0]:
        copy.wait_recv()
    sources[BLK : 2 * BLK, :] = vec_q[...].astype(BF16)
    for k in (0, 2):
        field = (halo[1, k].astype(F32) - (energy_now * scale) * halo[0, k].astype(F32)) * inverse
        sources[k * BLK : (k + 1) * BLK, :] = field.astype(BF16)
    apply()
    halo[2, 1] = vec_t[...].astype(BF16)
    for copy in halos[1]:
        copy.start()
    q, t, psi, im = vec_q[...], vec_t[...], start_buf[...], vec_im[...]
    red_drain(0)
    red_start(0, 0, dot_rows([(q, q), (q, im), (q, t), (psi, t)]))
    totals = red_total(0)

    def rotation(energy, coupling, curvature):
        x = 0.5 * (curvature - energy)
        size = jnp.maximum(jnp.abs(x), jnp.abs(coupling))
        safe = jnp.where(size > 0.0, size, 1.0)
        xs, ys = x / safe, -coupling / safe
        radius = jnp.sqrt(xs * xs + ys * ys)
        radius = jnp.where(size > 0.0, radius, 1.0)
        cos2 = jnp.where(size > 0.0, xs / radius, 1.0)
        sin2 = ys / radius
        big = jnp.sqrt(0.5 + 0.5 * jnp.abs(cos2))
        small = 0.5 * sin2 / big
        sign = jnp.where(coupling < 0.0, 1.0, -1.0)
        cosine = jnp.where(cos2 >= 0.0, big, jnp.abs(small))
        sine = jnp.where(cos2 >= 0.0, small, sign * big)
        lowest = 0.5 * (energy + curvature) - jnp.sqrt(x * x + coupling * coupling)
        return cosine, sine, lowest

    def kappa_of(square):
        return unit / jnp.sqrt(unit * unit * square + EPSILON)

    kappa = kappa_of(scalar(totals, 0))
    coupling = kappa * scalar(totals, 1)
    curvature = kappa * kappa * scalar(totals, 2)
    mirrored = kappa * scalar(totals, 3)
    cosine, sine, _ = rotation(energy_now, coupling, curvature)
    energy_next = (
        cosine * cosine * energy_now + cosine * sine * (coupling + mirrored) + sine * sine * curvature
    )
    turn = sine * kappa
    psi = cosine * start_buf[...] + turn * vec_q[...]
    im = cosine * vec_im[...] + turn * vec_t[...]
    start_buf[...] = psi
    vec_im[...] = im
    q = (im - energy_next * psi) * inverse
    vec_q[...] = q
    sources[BLK : 2 * BLK, :] = q.astype(BF16)

    for copy in halos[1]:
        copy.wait_recv()
    for k in (0, 2):
        h_psi = halo[0, k].astype(F32) * scale
        h_im = halo[1, k].astype(F32)
        h_q = (h_im - energy_now * h_psi) * inverse
        n_psi = cosine * h_psi + turn * h_q
        n_im = cosine * h_im + turn * halo[2, k].astype(F32)
        sources[k * BLK : (k + 1) * BLK, :] = ((n_im - energy_next * n_psi) * inverse).astype(BF16)
    apply()
    q, t, im = vec_q[...], vec_t[...], vec_im[...]
    red_drain(1)
    red_start(1, 0, dot_rows([(q, q), (q, im), (q, t)]))
    totals = red_total(1)
    kappa = kappa_of(scalar(totals, 0))
    coupling = kappa * scalar(totals, 1)
    curvature = kappa * kappa * scalar(totals, 2)
    cosine, sine, lowest = rotation(energy_next, coupling, curvature)
    psi_ref[0] = cosine * start_buf[...] + (sine * kappa) * vec_q[...]
    energy_ref[...] = jnp.broadcast_to(lowest, (1, 128))

    red_drain(0)
    red_drain(1)
    outgoing.wait_send()
    for copies in [start_halo] + halos:
        for copy in copies:
            copy.wait_send()


def body(wavefunction, environments, mpo_terms, sector_dims, channel_charges):
    vmem = pl.BlockSpec(memory_space=pltpu.VMEM)
    smem = pl.BlockSpec(memory_space=pltpu.SMEM)
    psi, energy = pl.pallas_call(
        kernel,
        out_shape=(
            jax.ShapeDtypeStruct((1, BLK, WIDTH), F32),
            jax.ShapeDtypeStruct((1, 128), F32),
        ),
        in_specs=[vmem, pl.BlockSpec(memory_space=pl.ANY), vmem, smem, smem],
        out_specs=(vmem, vmem),
        scratch_shapes=[
            pltpu.VMEM((2, CHAN, BLK * BLK), BF16),
            pltpu.VMEM((2, CHAN * BLK, 128), F32),
            pltpu.VMEM((CHAN * BLK, 3 * BLK), BF16),
            pltpu.VMEM((CHAN, 256, 256), BF16),
            pltpu.VMEM((CHAN, 256, 256), BF16),
            pltpu.VMEM((CHAN, 256, 256), BF16),
            pltpu.VMEM((8, 128), F32),
            pltpu.VMEM((256, 256), F32),
            pltpu.VMEM((3 * BLK, WIDTH), BF16),
            pltpu.VMEM((3, 3, BLK, WIDTH), BF16),
            pltpu.VMEM((BLK, 128), F32),
            pltpu.VMEM((BLK, WIDTH), F32),
            pltpu.VMEM((BLK, WIDTH), F32),
            pltpu.VMEM((BLK, WIDTH), F32),
            pltpu.VMEM((BLK, WIDTH), F32),
            pltpu.VMEM((2, SLOTS, 8, 128), F32),
            pltpu.SemaphoreType.DMA,
            pltpu.SemaphoreType.DMA((2,)),
            pltpu.SemaphoreType.DMA((3, 2)),
            pltpu.SemaphoreType.DMA((3, 2)),
            pltpu.SemaphoreType.DMA((2, len(GROUPS))),
            pltpu.SemaphoreType.DMA((2, len(GROUPS))),
        ],
        compiler_params=pltpu.CompilerParams(
            collective_id=0, has_side_effects=True, vmem_limit_bytes=48 * 2**20
        ),
    )(wavefunction, environments, mpo_terms, sector_dims, channel_charges)
    return psi, energy[0, :1]


def solution(mesh):
    return jax.shard_map(
        body,
        mesh=mesh,
        in_specs=(
            P(("section", "inner"), None, None),
            P(("section", "inner"), None, None),
            P(),
            P(("section", "inner"), None),
            P(),
        ),
        out_specs=(P(("section", "inner"), None, None), P("section")),
        check_vma=False,
    )
```

```python
import functools

import jax
import jax.numpy as jnp
from jax import lax
from jax.experimental import pallas as pl
from jax.experimental.pallas import tpu as pltpu
from jax.sharding import PartitionSpec as P

MESH = pl.DeviceIdType.MESH
F32 = jnp.float32
BF16 = jnp.bfloat16

ITERS = 2
EPSILON = 1e-06
BLK = 64
CHAN = 34
PH = 16
WIDTH = PH * BLK
PAIRS = BLK // 2

NEAR = tuple((0, d) for d in range(8))
ACROSS = ((0, 0), (0, 8), (1, 0), (1, 8))
EVERY = tuple((h, d) for h in (0, 1) for d in range(16))

CHUNKS = ((0, 12), (12, 24), (24, CHAN))
GROUP = 6


def flipped(index, bits):
    for bit in (1, 2, 4, 8):
        if bits & bit:
            index = index + bit * (1 - 2 * ((index // bit) % 2))
    return index


def low_half(rows):
    return lax.broadcasted_iota(jnp.int32, (rows, 128), 1) < BLK


def interchange(a, b, low):
    turned_a = pltpu.roll(a, BLK, 1)
    turned_b = pltpu.roll(b, BLK, 1)
    return jnp.where(low, a, turned_b), jnp.where(low, turned_a, b)


def to_mixed(field):
    low = low_half(16)
    rows = []
    for j in range(PH // 2):
        even, odd = [], []
        for p in range(2):
            a = field[32 * p : 32 * p + 16, 128 * j : 128 * j + 128]
            b = field[32 * p + 16 : 32 * p + 32, 128 * j : 128 * j + 128]
            first, second = interchange(a, b, low)
            even.append(first)
            odd.append(second)
        rows.append(jnp.concatenate(even, axis=1))
        rows.append(jnp.concatenate(odd, axis=1))
    return jnp.concatenate(rows, axis=0)


def kernel(
    wave_ref, env_ref, mpo_ref, dims_ref, charge_ref, psi_ref, energy_ref,
    env_buf, wide, raw, outgoing, lsel, rsel, wsel, image, sources,
    halo, mask, columns, start_buf, vec_im, vec_q, vec_t, near_buf, exchange,
    env_load, env_send, env_recv, halo_send, halo_recv, near_send, near_recv, red_send, red_recv,
):
    section, inner = lax.axis_index("section"), lax.axis_index("inner")
    n_inner = lax.axis_size("inner")
    parity = section % 2
    even = parity == 0
    entries = 2.0 * n_inner * BLK * WIDTH

    def at(h, d):
        return (flipped(section, h), flipped(inner, d))

    above = (section, (inner + 1) % n_inner)
    below = (section, (inner + n_inner - 1) % n_inner)
    partner = at(1, 0)

    peers = [partner, above, below] + [at(h, d) for h, d in NEAR[1:] + ACROSS[1:2] + ACROSS[3:]]
    barrier = pltpu.get_barrier_semaphore()
    for peer in peers:
        pl.semaphore_signal(barrier, inc=1, device_id=peer, device_id_type=MESH)

    def env_rows(k, factor):
        first, last = CHUNKS[k]
        return pl.ds(first * PAIRS * factor, (last - first) * PAIRS * factor)

    loads = [
        pltpu.make_async_copy(env_ref.at[env_rows(k, 2)], env_buf.at[env_rows(k, 2)], env_load.at[k])
        for k in range(len(CHUNKS))
    ]
    for load in loads:
        load.start()

    row8 = lax.broadcasted_iota(jnp.int32, (8, 128), 0)
    lane8 = lax.broadcasted_iota(jnp.int32, (8, 128), 1)

    def dots(pairs):
        packed = jnp.zeros((8, 128), F32)
        for k, (x, y) in enumerate(pairs):
            prod = x * y
            tiles = [
                prod[8 * i : 8 * i + 8, 128 * j : 128 * j + 128] for i in range(BLK // 8) for j in range(WIDTH // 128)
            ]
            while len(tiles) > 1:
                tiles = [tiles[2 * n] + tiles[2 * n + 1] for n in range(len(tiles) // 2)]
            tile = tiles[0] + pltpu.roll(tiles[0], 64, 1)
            tile = tile + pltpu.roll(tile, 32, 1)
            packed = jnp.where(lane8 // 32 == k, tile, packed)
        return jnp.sum(packed, axis=0, keepdims=True)

    def send_row(buf, group, value, send, recv):
        buf[0:1, :] = value
        for j, (h, d) in enumerate(group[1:]):
            pltpu.make_async_remote_copy(
                src_ref=buf.at[pl.ds(0, 1)],
                dst_ref=buf.at[pl.ds(j + 1, 1)],
                send_sem=send,
                recv_sem=recv,
                device_id=at(h, d),
                device_id_type=MESH,
            ).start()

    def await_rows(buf, group, sem):
        rows = buf.at[pl.ds(1, len(group) - 1)]
        pltpu.make_async_copy(rows, rows, sem).wait()

    def total_rows(tile):
        for step in (4, 2, 1):
            tile = tile + pltpu.roll(tile, step, 0)
        return tile

    def scalars(tile):
        return jnp.sum(jnp.where(lane8 // 32 == row8, tile, 0.0), axis=1, keepdims=True) * (1.0 / entries)

    def sum_start(k, pairs):
        send_row(exchange.at[k], EVERY, dots(pairs), red_send.at[k], red_recv.at[k])

    def sum_finish(k):
        await_rows(exchange.at[k], EVERY, red_recv.at[k])
        part = [exchange[k, 8 * n : 8 * n + 8, :] for n in range(4)]
        return scalars(total_rows((part[0] + part[1]) + (part[2] + part[3])))

    def halo_copies(k):
        return [
            pltpu.make_async_remote_copy(
                src_ref=halo.at[k, 1],
                dst_ref=halo.at[k, 2 * side],
                send_sem=halo_send.at[k, side],
                recv_sem=halo_recv.at[k, side],
                device_id=target,
                device_id_type=MESH,
            )
            for side, target in ((0, above), (1, below))
        ]

    def channels(first, last):
        groups = [(a, min(a + GROUP, last)) for a in range(first, last, GROUP)]

        def left(group):
            a, b = group
            out = jnp.dot(lsel[a * BLK : b * BLK, :], sources[...], preferred_element_type=F32).astype(BF16)
            return [to_mixed(out[k * BLK : (k + 1) * BLK]) for k in range(b - a)]

        total = None
        ready = left(groups[0])
        for n, (a, b) in enumerate(groups):
            now = ready
            if n + 1 < len(groups):
                ready = left(groups[n + 1])
            mixed = [
                jnp.dot(wsel[a + k], now[k], preferred_element_type=F32).astype(BF16) for k in range(b - a)
            ]
            right = rsel[a:b].reshape((b - a) * 256, 256)
            part = jnp.dot(jnp.concatenate(mixed, axis=1), right, preferred_element_type=F32)
            total = part if total is None else total + part
        return total

    def unmix(total):
        low = low_half(16)
        for j in range(PH // 2):
            for p in range(2):
                a = total[32 * j : 32 * j + 16, 128 * p : 128 * p + 128]
                b = total[32 * j + 16 : 32 * j + 32, 128 * p : 128 * p + 128]
                upper, lower = interchange(a, b, low)
                columns[j, pl.ds(p, 16, stride=2), :] = upper
                columns[j, pl.ds(32 + p, 16, stride=2), :] = lower
        for j in range(PH // 2):
            vec_t[:, 128 * j : 128 * j + 128] = columns[j] * mask[...]

    row = lax.broadcasted_iota(jnp.int32, (BLK, 128), 0)
    lane = lax.broadcasted_iota(jnp.int32, (BLK, 128), 1)
    live = (row < dims_ref[0, 0]) & (lane % BLK < dims_ref[0, 1])
    mask[...] = jnp.where(live, 1.0, 0.0).astype(F32)
    start = wave_ref[0] * jnp.concatenate([mask[...]] * (WIDTH // 128), axis=1)
    start_buf[...] = start
    halo[0, 1] = start.astype(BF16)
    norm_row = dots([(start, start)])

    for k in range(len(CHUNKS)):
        loads[k].wait()
        wide[env_rows(k, 2), :] = env_buf[env_rows(k, 2), :].astype(F32)
        first, last = CHUNKS[k]
        count = (last - first) * PAIRS
        upper = wide[pl.ds(first * PAIRS * 2, count, stride=2), :]
        lower = wide[pl.ds(first * PAIRS * 2 + 1, count, stride=2), :]
        raw[parity, env_rows(k, 1), :] = jnp.where(even, upper, lower).astype(BF16)
        outgoing[env_rows(k, 1), :] = jnp.where(even, lower, upper).astype(BF16)

    pl.semaphore_wait(barrier, len(peers))
    env_copies = [
        pltpu.make_async_remote_copy(
            src_ref=outgoing.at[env_rows(k, 1)],
            dst_ref=raw.at[parity, env_rows(k, 1)],
            send_sem=env_send.at[k],
            recv_sem=env_recv.at[k],
            device_id=partner,
            device_id_type=MESH,
        )
        for k in range(len(CHUNKS))
    ]
    start_halo = halo_copies(0)
    env_copies[0].start()
    for copy in start_halo:
        copy.start()
    for copy in env_copies[1:]:
        copy.start()
    send_row(near_buf.at[0], NEAR, norm_row, near_send.at[0], near_recv.at[0])

    def iota(shape, axis):
        return lax.broadcasted_iota(jnp.int32, shape, axis)

    flat = mpo_ref[...].reshape(PH * PH, CHAN)
    unit_rows = (iota((CHAN, CHAN), 0) == iota((CHAN, CHAN), 1)).astype(BF16)
    by_channel = lax.dot_general(unit_rows, flat, (((1,), (1,)), ((), ())), preferred_element_type=F32)
    keep_t = iota((PH, 256), 1) % 16 == iota((PH, 256), 0)
    picked = jnp.concatenate(
        [jnp.where(keep_t, jnp.broadcast_to(by_channel[a : a + 1, :], (PH, 256)), 0.0) for a in range(CHAN)], axis=0
    ).astype(BF16)
    widen = (iota((256, 256), 0) // 16 == iota((256, 256), 1) // 16).astype(BF16)
    terms = jnp.dot(picked, widen, preferred_element_type=F32).astype(BF16)
    spread_rows = (iota((256, PH), 0) // 16 == iota((256, PH), 1)).astype(BF16)
    same = iota((256, 256), 0) % 16 == iota((256, 256), 1) % 16
    for a in range(CHAN):
        both = jnp.dot(spread_rows, terms[a * PH : (a + 1) * PH], preferred_element_type=F32)
        wsel[a] = jnp.where(same, both, 0.0).astype(BF16)

    low32 = low_half(32)
    low64 = low_half(64)

    def doubled(slot, a):
        x = raw[slot, a * PAIRS : (a + 1) * PAIRS, :]
        turned = pltpu.roll(x, BLK, 1)
        return jnp.where(low32, x, turned), jnp.where(low32, turned, x)

    def place_left(first, last):
        for a in range(first, last):
            charge = charge_ref[a]
            here = jnp.where(low32, -1, 0) == charge
            there = jnp.logical_and(low32, charge == 1)
            for half, value in enumerate(doubled(0, a)):
                rows = slice(a * BLK + half * PAIRS, a * BLK + (half + 1) * PAIRS)
                none = jnp.zeros_like(value)
                lsel[rows, 0:128] = jnp.where(here, value, none)
                lsel[rows, 128:192] = jnp.where(there, value, none)[:, :BLK]

    def place_right(first, last):
        none = jnp.zeros((BLK, 128), BF16)
        zero = jnp.zeros((2 * BLK, 128), BF16)
        for a in range(first, last):
            upper, lower = doubled(1, a)
            wide[pl.ds(a * BLK, PAIRS, stride=2), :] = upper.astype(F32)
            wide[pl.ds(a * BLK + 1, PAIRS, stride=2), :] = lower.astype(F32)
            both = wide[a * BLK : (a + 1) * BLK, :].astype(BF16)
            block = jnp.concatenate([jnp.where(low64, both, none), jnp.where(low64, none, both)], axis=0)
            rsel[a, 0:128, 0:128] = block
            rsel[a, 128:256, 128:256] = block
            rsel[a, 0:128, 128:256] = zero
            rsel[a, 128:256, 0:128] = zero

    @pl.when(even)
    def _():
        place_left(0, CHAN)

    @pl.when(jnp.logical_not(even))
    def _():
        place_right(0, CHAN)

    await_rows(near_buf.at[0], NEAR, near_recv.at[0])
    norm_row = total_rows(near_buf[0])[0:1, :]
    send_row(near_buf.at[1], ACROSS, norm_row, near_send.at[1], near_recv.at[1])

    for copy in start_halo:
        copy.wait_recv()
    for k in range(3):
        sources[k * BLK : (k + 1) * BLK, :] = halo[0, k]
    total = None
    for k, (first, last) in enumerate(CHUNKS):
        arrived = raw.at[1 - parity, env_rows(k, 1)]
        pltpu.make_async_copy(arrived, arrived, env_recv.at[k]).wait()

        @pl.when(even)
        def _():
            place_right(first, last)

        @pl.when(jnp.logical_not(even))
        def _():
            place_left(first, last)

        if k:
            image[...] += channels(first, last)
        else:
            image[...] = channels(first, last)

    await_rows(near_buf.at[1], ACROSS, near_recv.at[1])
    part = [near_buf[1, k : k + 1, :] for k in range(4)]
    norm_row = (part[0] + part[1]) + (part[2] + part[3])
    norm = jnp.sum(jnp.where(lane8[0:1] < 32, norm_row, 0.0), axis=1, keepdims=True) * (1.0 / entries)
    scale = 1.0 / jnp.sqrt(norm + EPSILON)
    unmix(image[...])
    im = vec_t[...] * scale
    vec_im[...] = im
    halo[1, 1] = im.astype(BF16)
    halos = [halo_copies(1), halo_copies(2)]
    for copy in halos[0]:
        copy.start()
    psi = start_buf[...] * scale
    start_buf[...] = psi
    sum_start(0, [(psi, im), (im, im)])
    totals = sum_finish(0)

    def scalar(total, k):
        return total[k : k + 1, :]

    energy_now = scalar(totals, 0)
    unit = jnp.sqrt(scalar(totals, 1) + EPSILON)
    inverse = 1.0 / unit

    vec_q[...] = (vec_im[...] - energy_now * start_buf[...]) * inverse
    for copy in halos[0]:
        copy.wait_recv()
    sources[BLK : 2 * BLK, :] = vec_q[...].astype(BF16)
    for k in (0, 2):
        field = (halo[1, k].astype(F32) - (energy_now * scale) * halo[0, k].astype(F32)) * inverse
        sources[k * BLK : (k + 1) * BLK, :] = field.astype(BF16)
    unmix(channels(0, CHAN))
    halo[2, 1] = vec_t[...].astype(BF16)
    for copy in halos[1]:
        copy.start()
    q, t, psi, im = vec_q[...], vec_t[...], start_buf[...], vec_im[...]
    sum_start(1, [(q, q), (q, im), (q, t), (psi, t)])
    totals = sum_finish(1)

    def rotation(energy, coupling, curvature):
        x = 0.5 * (curvature - energy)
        size = jnp.maximum(jnp.abs(x), jnp.abs(coupling))
        safe = jnp.where(size > 0.0, size, 1.0)
        xs, ys = x / safe, -coupling / safe
        radius = jnp.sqrt(xs * xs + ys * ys)
        radius = jnp.where(size > 0.0, radius, 1.0)
        cos2 = jnp.where(size > 0.0, xs / radius, 1.0)
        sin2 = ys / radius
        big = jnp.sqrt(0.5 + 0.5 * jnp.abs(cos2))
        small = 0.5 * sin2 / big
        sign = jnp.where(coupling < 0.0, 1.0, -1.0)
        cosine = jnp.where(cos2 >= 0.0, big, jnp.abs(small))
        sine = jnp.where(cos2 >= 0.0, small, sign * big)
        lowest = 0.5 * (energy + curvature) - jnp.sqrt(x * x + coupling * coupling)
        return cosine, sine, lowest

    def kappa_of(square):
        return unit / jnp.sqrt(unit * unit * square + EPSILON)

    kappa = kappa_of(scalar(totals, 0))
    coupling = kappa * scalar(totals, 1)
    curvature = kappa * kappa * scalar(totals, 2)
    mirrored = kappa * scalar(totals, 3)
    cosine, sine, _ = rotation(energy_now, coupling, curvature)
    energy_next = (
        cosine * cosine * energy_now + cosine * sine * (coupling + mirrored) + sine * sine * curvature
    )
    turn = sine * kappa
    psi = cosine * start_buf[...] + turn * vec_q[...]
    im = cosine * vec_im[...] + turn * vec_t[...]
    start_buf[...] = psi
    vec_im[...] = im
    q = (im - energy_next * psi) * inverse
    vec_q[...] = q
    sources[BLK : 2 * BLK, :] = q.astype(BF16)

    for copy in halos[1]:
        copy.wait_recv()
    for k in (0, 2):
        h_psi = halo[0, k].astype(F32) * scale
        h_im = halo[1, k].astype(F32)
        h_q = (h_im - energy_now * h_psi) * inverse
        n_psi = cosine * h_psi + turn * h_q
        n_im = cosine * h_im + turn * halo[2, k].astype(F32)
        sources[k * BLK : (k + 1) * BLK, :] = ((n_im - energy_next * n_psi) * inverse).astype(BF16)
    unmix(channels(0, CHAN))
    q, t, im = vec_q[...], vec_t[...], vec_im[...]
    sum_start(2, [(q, q), (q, im), (q, t)])
    totals = sum_finish(2)
    kappa = kappa_of(scalar(totals, 0))
    coupling = kappa * scalar(totals, 1)
    curvature = kappa * kappa * scalar(totals, 2)
    cosine, sine, lowest = rotation(energy_next, coupling, curvature)
    psi_ref[0] = cosine * start_buf[...] + (sine * kappa) * vec_q[...]
    energy_ref[...] = jnp.broadcast_to(lowest, (1, 128))

    await_rows(near_buf.at[0], NEAR, near_send.at[0])
    await_rows(near_buf.at[1], ACROSS, near_send.at[1])
    for k in range(3):
        await_rows(exchange.at[k], EVERY, red_send.at[k])
    for copies in [env_copies, start_halo] + halos:
        for copy in copies:
            copy.wait_send()


def body(wavefunction, environments, mpo_terms, sector_dims, channel_charges):
    rows = environments.reshape(2, CHAN, PAIRS, 128).transpose(1, 2, 0, 3).reshape(CHAN * PAIRS * 2, 128)
    terms = mpo_terms.transpose(1, 2, 0)
    vmem = pl.BlockSpec(memory_space=pltpu.VMEM)
    smem = pl.BlockSpec(memory_space=pltpu.SMEM)
    psi, energy = pl.pallas_call(
        kernel,
        out_shape=(
            jax.ShapeDtypeStruct((1, BLK, WIDTH), F32),
            jax.ShapeDtypeStruct((1, 128), F32),
        ),
        in_specs=[vmem, pl.BlockSpec(memory_space=pl.ANY), vmem, smem, smem],
        out_specs=(vmem, vmem),
        scratch_shapes=[
            pltpu.VMEM((2 * CHAN * PAIRS, 128), BF16),
            pltpu.VMEM((2 * CHAN * PAIRS, 128), F32),
            pltpu.VMEM((2, CHAN * PAIRS, 128), BF16),
            pltpu.VMEM((CHAN * PAIRS, 128), BF16),
            pltpu.VMEM((CHAN * BLK, 3 * BLK), BF16),
            pltpu.VMEM((CHAN, 256, 256), BF16),
            pltpu.VMEM((CHAN, 256, 256), BF16),
            pltpu.VMEM((256, 256), F32),
            pltpu.VMEM((3 * BLK, WIDTH), BF16),
            pltpu.VMEM((3, 3, BLK, WIDTH), BF16),
            pltpu.VMEM((BLK, 128), F32),
            pltpu.VMEM((PH // 2, BLK, 128), F32),
            pltpu.VMEM((BLK, WIDTH), F32),
            pltpu.VMEM((BLK, WIDTH), F32),
            pltpu.VMEM((BLK, WIDTH), F32),
            pltpu.VMEM((BLK, WIDTH), F32),
            pltpu.VMEM((2, 8, 128), F32),
            pltpu.VMEM((3, 32, 128), F32),
            pltpu.SemaphoreType.DMA((len(CHUNKS),)),
            pltpu.SemaphoreType.DMA((len(CHUNKS),)),
            pltpu.SemaphoreType.DMA((len(CHUNKS),)),
            pltpu.SemaphoreType.DMA((3, 2)),
            pltpu.SemaphoreType.DMA((3, 2)),
            pltpu.SemaphoreType.DMA((2,)),
            pltpu.SemaphoreType.DMA((2,)),
            pltpu.SemaphoreType.DMA((3,)),
            pltpu.SemaphoreType.DMA((3,)),
        ],
        compiler_params=pltpu.CompilerParams(
            collective_id=0, has_side_effects=True, vmem_limit_bytes=60 * 2**20
        ),
    )(wavefunction, rows, terms, sector_dims, channel_charges)
    return psi, energy[0, :1]


def solution(mesh):
    return jax.shard_map(
        body,
        mesh=mesh,
        in_specs=(
            P(("section", "inner"), None, None),
            P(("section", "inner"), None, None),
            P(),
            P(("section", "inner"), None),
            P(),
        ),
        out_specs=(P(("section", "inner"), None, None), P("section")),
        check_vma=False,
    )
```

```python
import functools

import jax
import jax.numpy as jnp
from jax import lax
from jax.experimental import pallas as pl
from jax.experimental.pallas import tpu as pltpu
from jax.sharding import PartitionSpec as P

MESH = pl.DeviceIdType.MESH
F32 = jnp.float32
BF16 = jnp.bfloat16

ITERS = 2
EPSILON = 1e-06
BLK = 64
CHAN = 34
PH = 16
WIDTH = PH * BLK
PAIRS = BLK // 2

NEAR = tuple((0, d) for d in range(8))
ACROSS = ((0, 0), (0, 8), (1, 0), (1, 8))
EVERY = tuple((h, d) for h in (0, 1) for d in range(16))


def distance(peer):
    h, d = peer
    return h + (d & 8) // 8 + (2 if d & 6 == 4 else 1 if d & 6 else 0)


CHUNKS = ((0, 12), (12, 24), (24, CHAN))
GROUP = 4


def flipped(index, bits):
    for bit in (1, 2, 4, 8):
        if bits & bit:
            index = index + bit * (1 - 2 * ((index // bit) % 2))
    return index


def low_half(rows):
    return lax.broadcasted_iota(jnp.int32, (rows, 128), 1) < BLK


def interchange(a, b, low):
    turned_a = pltpu.roll(a, BLK, 1)
    turned_b = pltpu.roll(b, BLK, 1)
    return jnp.where(low, a, turned_b), jnp.where(low, turned_a, b)


def to_mixed(field):
    low = low_half(16)
    rows = []
    for j in range(PH // 2):
        even, odd = [], []
        for p in range(2):
            a = field[32 * p : 32 * p + 16, 128 * j : 128 * j + 128]
            b = field[32 * p + 16 : 32 * p + 32, 128 * j : 128 * j + 128]
            first, second = interchange(a, b, low)
            even.append(first)
            odd.append(second)
        rows.append(jnp.concatenate(even, axis=1))
        rows.append(jnp.concatenate(odd, axis=1))
    return jnp.concatenate(rows, axis=0)


def kernel(
    wave_hbm, env_ref, mpo_hbm, dims_hbm, charge_hbm, psi_ref, energy_ref,
    wave_ref, mpo_ref, dims_ref, charge_ref, env_buf, wide, raw, outgoing, lsel, rsel, wsel, image, sources,
    halo, mask, columns, start_buf, vec_im, vec_q, vec_t, near_buf, exchange,
    small_load, env_load, env_send, env_recv, halo_send, halo_recv, near_send, near_recv, red_send, red_recv,
):
    section, inner = lax.axis_index("section"), lax.axis_index("inner")
    n_inner = lax.axis_size("inner")
    parity = section % 2
    even = parity == 0
    entries = 2.0 * n_inner * BLK * WIDTH

    def at(h, d):
        return (flipped(section, h), flipped(inner, d))

    above = (section, (inner + 1) % n_inner)
    below = (section, (inner + n_inner - 1) % n_inner)
    partner = at(1, 0)

    peers = [partner, above, below] + [at(h, d) for h, d in NEAR[1:] + ACROSS[1:2] + ACROSS[3:]]
    barrier = pltpu.get_barrier_semaphore()
    for peer in peers:
        pl.semaphore_signal(barrier, inc=1, device_id=peer, device_id_type=MESH)

    small = [
        pltpu.make_async_copy(source, target, small_load.at[k])
        for k, (source, target) in enumerate(
            ((dims_hbm, dims_ref), (wave_hbm, wave_ref), (mpo_hbm, mpo_ref), (charge_hbm, charge_ref))
        )
    ]
    small[0].start()
    small[1].start()

    def env_rows(k, factor):
        first, last = CHUNKS[k]
        return pl.ds(first * PAIRS * factor, (last - first) * PAIRS * factor)

    loads = [
        pltpu.make_async_copy(env_ref.at[env_rows(k, 2)], env_buf.at[env_rows(k, 2)], env_load.at[k])
        for k in range(len(CHUNKS))
    ]
    for load in loads + small[2:]:
        load.start()

    row8 = lax.broadcasted_iota(jnp.int32, (8, 128), 0)
    lane8 = lax.broadcasted_iota(jnp.int32, (8, 128), 1)

    def dots(pairs):
        packed = jnp.zeros((8, 128), F32)
        for k, (x, y) in enumerate(pairs):
            prod = x * y
            tiles = [
                prod[8 * i : 8 * i + 8, 128 * j : 128 * j + 128] for i in range(BLK // 8) for j in range(WIDTH // 128)
            ]
            while len(tiles) > 1:
                tiles = [tiles[2 * n] + tiles[2 * n + 1] for n in range(len(tiles) // 2)]
            tile = tiles[0] + pltpu.roll(tiles[0], 64, 1)
            tile = tile + pltpu.roll(tile, 32, 1)
            packed = jnp.where(lane8 // 32 == k, tile, packed)
        return jnp.sum(packed, axis=0, keepdims=True)

    def send_row(buf, group, value, send, recv):
        buf[0:1, :] = value
        for h, d in sorted(group[1:], key=distance, reverse=True):
            j = group.index((h, d))
            pltpu.make_async_remote_copy(
                src_ref=buf.at[pl.ds(0, 1)],
                dst_ref=buf.at[pl.ds(j, 1)],
                send_sem=send,
                recv_sem=recv,
                device_id=at(h, d),
                device_id_type=MESH,
            ).start()

    def await_rows(buf, group, sem):
        rows = buf.at[pl.ds(1, len(group) - 1)]
        pltpu.make_async_copy(rows, rows, sem).wait()

    def total_rows(tile):
        for step in (4, 2, 1):
            tile = tile + pltpu.roll(tile, step, 0)
        return tile

    def scalars(tile):
        return jnp.sum(jnp.where(lane8 // 32 == row8, tile, 0.0), axis=1, keepdims=True) * (1.0 / entries)

    def sum_start(k, pairs):
        send_row(exchange.at[k], EVERY, dots(pairs), red_send.at[k], red_recv.at[k])

    def sum_finish(k):
        await_rows(exchange.at[k], EVERY, red_recv.at[k])
        part = [exchange[k, 8 * n : 8 * n + 8, :] for n in range(4)]
        return scalars(total_rows((part[0] + part[1]) + (part[2] + part[3])))

    def halo_copies(k):
        return [
            pltpu.make_async_remote_copy(
                src_ref=halo.at[k, 1],
                dst_ref=halo.at[k, 2 * side],
                send_sem=halo_send.at[k, side],
                recv_sem=halo_recv.at[k, side],
                device_id=target,
                device_id_type=MESH,
            )
            for side, target in ((0, above), (1, below))
        ]

    def channels(first, last):
        groups = [(a, min(a + GROUP, last)) for a in range(first, last, GROUP)]

        def left(group):
            a, b = group
            out = jnp.dot(lsel[a * BLK : b * BLK, :], sources[...], preferred_element_type=F32).astype(BF16)
            return [to_mixed(out[k * BLK : (k + 1) * BLK]) for k in range(b - a)]

        total = None
        ready = left(groups[0])
        for n, (a, b) in enumerate(groups):
            now = ready
            if n + 1 < len(groups):
                ready = left(groups[n + 1])
            mixed = [
                jnp.dot(wsel[a + k], now[k], preferred_element_type=F32).astype(BF16) for k in range(b - a)
            ]
            right = rsel[a:b].reshape((b - a) * 256, 256)
            part = jnp.dot(jnp.concatenate(mixed, axis=1), right, preferred_element_type=F32)
            total = part if total is None else total + part
        return total

    def unmix(total):
        low = low_half(16)
        for j in range(PH // 2):
            for p in range(2):
                a = total[32 * j : 32 * j + 16, 128 * p : 128 * p + 128]
                b = total[32 * j + 16 : 32 * j + 32, 128 * p : 128 * p + 128]
                upper, lower = interchange(a, b, low)
                columns[j, pl.ds(p, 16, stride=2), :] = upper
                columns[j, pl.ds(32 + p, 16, stride=2), :] = lower
        for j in range(PH // 2):
            vec_t[:, 128 * j : 128 * j + 128] = columns[j] * mask[...]

    small[0].wait()
    small[1].wait()
    row = lax.broadcasted_iota(jnp.int32, (BLK, 128), 0)
    lane = lax.broadcasted_iota(jnp.int32, (BLK, 128), 1)
    live = (row < dims_ref[0, 0]) & (lane % BLK < dims_ref[0, 1])
    mask[...] = jnp.where(live, 1.0, 0.0).astype(F32)
    start = wave_ref[0] * jnp.concatenate([mask[...]] * (WIDTH // 128), axis=1)
    start_buf[...] = start
    halo[0, 1] = start.astype(BF16)
    norm_row = dots([(start, start)])

    for k in range(len(CHUNKS)):
        loads[k].wait()
        wide[env_rows(k, 2), :] = env_buf[env_rows(k, 2), :].astype(F32)
        first, last = CHUNKS[k]
        count = (last - first) * PAIRS
        upper = wide[pl.ds(first * PAIRS * 2, count, stride=2), :]
        lower = wide[pl.ds(first * PAIRS * 2 + 1, count, stride=2), :]
        raw[parity, env_rows(k, 1), :] = jnp.where(even, upper, lower).astype(BF16)
        outgoing[env_rows(k, 1), :] = jnp.where(even, lower, upper).astype(BF16)

    pl.semaphore_wait(barrier, len(peers))
    env_copies = [
        pltpu.make_async_remote_copy(
            src_ref=outgoing.at[env_rows(k, 1)],
            dst_ref=raw.at[parity, env_rows(k, 1)],
            send_sem=env_send.at[k],
            recv_sem=env_recv.at[k],
            device_id=partner,
            device_id_type=MESH,
        )
        for k in range(len(CHUNKS))
    ]
    start_halo = halo_copies(0)
    env_copies[0].start()
    for copy in start_halo:
        copy.start()
    for copy in env_copies[1:]:
        copy.start()
    send_row(near_buf.at[0], NEAR, norm_row, near_send.at[0], near_recv.at[0])

    def iota(shape, axis):
        return lax.broadcasted_iota(jnp.int32, shape, axis)

    small[2].wait()
    small[3].wait()
    flat = mpo_ref[...].reshape(PH * PH, CHAN)
    unit_rows = (iota((CHAN, CHAN), 0) == iota((CHAN, CHAN), 1)).astype(BF16)
    by_channel = lax.dot_general(unit_rows, flat, (((1,), (1,)), ((), ())), preferred_element_type=F32)
    keep_t = iota((PH, 256), 1) % 16 == iota((PH, 256), 0)
    picked = jnp.concatenate(
        [jnp.where(keep_t, jnp.broadcast_to(by_channel[a : a + 1, :], (PH, 256)), 0.0) for a in range(CHAN)], axis=0
    ).astype(BF16)
    widen = (iota((256, 256), 0) // 16 == iota((256, 256), 1) // 16).astype(BF16)
    terms = jnp.dot(picked, widen, preferred_element_type=F32).astype(BF16)
    spread_rows = (iota((256, PH), 0) // 16 == iota((256, PH), 1)).astype(BF16)
    same = iota((256, 256), 0) % 16 == iota((256, 256), 1) % 16
    for a in range(CHAN):
        both = jnp.dot(spread_rows, terms[a * PH : (a + 1) * PH], preferred_element_type=F32)
        wsel[a] = jnp.where(same, both, 0.0).astype(BF16)

    low32 = low_half(32)
    low64 = low_half(64)

    def doubled(slot, a):
        x = raw[slot, a * PAIRS : (a + 1) * PAIRS, :]
        turned = pltpu.roll(x, BLK, 1)
        return jnp.where(low32, x, turned), jnp.where(low32, turned, x)

    def place_left(first, last):
        for a in range(first, last):
            charge = charge_ref[a]
            here = jnp.where(low32, -1, 0) == charge
            there = jnp.logical_and(low32, charge == 1)
            for half, value in enumerate(doubled(0, a)):
                rows = slice(a * BLK + half * PAIRS, a * BLK + (half + 1) * PAIRS)
                none = jnp.zeros_like(value)
                lsel[rows, 0:128] = jnp.where(here, value, none)
                lsel[rows, 128:192] = jnp.where(there, value, none)[:, :BLK]

    def place_right(first, last):
        none = jnp.zeros((BLK, 128), BF16)
        zero = jnp.zeros((2 * BLK, 128), BF16)
        for a in range(first, last):
            upper, lower = doubled(1, a)
            wide[pl.ds(a * BLK, PAIRS, stride=2), :] = upper.astype(F32)
            wide[pl.ds(a * BLK + 1, PAIRS, stride=2), :] = lower.astype(F32)
            both = wide[a * BLK : (a + 1) * BLK, :].astype(BF16)
            block = jnp.concatenate([jnp.where(low64, both, none), jnp.where(low64, none, both)], axis=0)
            rsel[a, 0:128, 0:128] = block
            rsel[a, 128:256, 128:256] = block
            rsel[a, 0:128, 128:256] = zero
            rsel[a, 128:256, 0:128] = zero

    @pl.when(even)
    def _():
        place_left(0, CHAN)

    @pl.when(jnp.logical_not(even))
    def _():
        place_right(0, CHAN)

    await_rows(near_buf.at[0], NEAR, near_recv.at[0])
    norm_row = total_rows(near_buf[0])[0:1, :]
    send_row(near_buf.at[1], ACROSS, norm_row, near_send.at[1], near_recv.at[1])

    for copy in start_halo:
        copy.wait_recv()
    for k in range(3):
        sources[k * BLK : (k + 1) * BLK, :] = halo[0, k]
    total = None
    for k, (first, last) in enumerate(CHUNKS):
        arrived = raw.at[1 - parity, env_rows(k, 1)]
        pltpu.make_async_copy(arrived, arrived, env_recv.at[k]).wait()

        @pl.when(even)
        def _():
            place_right(first, last)

        @pl.when(jnp.logical_not(even))
        def _():
            place_left(first, last)

        if k:
            image[...] += channels(first, last)
        else:
            image[...] = channels(first, last)

    await_rows(near_buf.at[1], ACROSS, near_recv.at[1])
    part = [near_buf[1, k : k + 1, :] for k in range(4)]
    norm_row = (part[0] + part[1]) + (part[2] + part[3])
    norm = jnp.sum(jnp.where(lane8[0:1] < 32, norm_row, 0.0), axis=1, keepdims=True) * (1.0 / entries)
    scale = 1.0 / jnp.sqrt(norm + EPSILON)
    unmix(image[...])
    im = vec_t[...] * scale
    vec_im[...] = im
    halo[1, 1] = im.astype(BF16)
    halos = [halo_copies(1), halo_copies(2)]
    for copy in halos[0]:
        copy.start()
    psi = start_buf[...] * scale
    start_buf[...] = psi
    sum_start(0, [(psi, im), (im, im)])
    totals = sum_finish(0)

    def scalar(total, k):
        return total[k : k + 1, :]

    energy_now = scalar(totals, 0)
    unit = jnp.sqrt(scalar(totals, 1) + EPSILON)
    inverse = 1.0 / unit

    vec_q[...] = (vec_im[...] - energy_now * start_buf[...]) * inverse
    for copy in halos[0]:
        copy.wait_recv()
    sources[BLK : 2 * BLK, :] = vec_q[...].astype(BF16)
    for k in (0, 2):
        field = (halo[1, k].astype(F32) - (energy_now * scale) * halo[0, k].astype(F32)) * inverse
        sources[k * BLK : (k + 1) * BLK, :] = field.astype(BF16)
    unmix(channels(0, CHAN))
    halo[2, 1] = vec_t[...].astype(BF16)
    for copy in halos[1]:
        copy.start()
    q, t, psi, im = vec_q[...], vec_t[...], start_buf[...], vec_im[...]
    sum_start(1, [(q, q), (q, im), (q, t), (psi, t)])
    totals = sum_finish(1)

    def rotation(energy, coupling, curvature):
        x = 0.5 * (curvature - energy)
        size = jnp.maximum(jnp.abs(x), jnp.abs(coupling))
        safe = jnp.where(size > 0.0, size, 1.0)
        xs, ys = x / safe, -coupling / safe
        radius = jnp.sqrt(xs * xs + ys * ys)
        radius = jnp.where(size > 0.0, radius, 1.0)
        cos2 = jnp.where(size > 0.0, xs / radius, 1.0)
        sin2 = ys / radius
        big = jnp.sqrt(0.5 + 0.5 * jnp.abs(cos2))
        small = 0.5 * sin2 / big
        sign = jnp.where(coupling < 0.0, 1.0, -1.0)
        cosine = jnp.where(cos2 >= 0.0, big, jnp.abs(small))
        sine = jnp.where(cos2 >= 0.0, small, sign * big)
        lowest = 0.5 * (energy + curvature) - jnp.sqrt(x * x + coupling * coupling)
        return cosine, sine, lowest

    def kappa_of(square):
        return unit / jnp.sqrt(unit * unit * square + EPSILON)

    kappa = kappa_of(scalar(totals, 0))
    coupling = kappa * scalar(totals, 1)
    curvature = kappa * kappa * scalar(totals, 2)
    mirrored = kappa * scalar(totals, 3)
    cosine, sine, _ = rotation(energy_now, coupling, curvature)
    energy_next = (
        cosine * cosine * energy_now + cosine * sine * (coupling + mirrored) + sine * sine * curvature
    )
    turn = sine * kappa
    psi = cosine * start_buf[...] + turn * vec_q[...]
    im = cosine * vec_im[...] + turn * vec_t[...]
    start_buf[...] = psi
    vec_im[...] = im
    q = (im - energy_next * psi) * inverse
    vec_q[...] = q
    sources[BLK : 2 * BLK, :] = q.astype(BF16)

    for copy in halos[1]:
        copy.wait_recv()
    for k in (0, 2):
        h_psi = halo[0, k].astype(F32) * scale
        h_im = halo[1, k].astype(F32)
        h_q = (h_im - energy_now * h_psi) * inverse
        n_psi = cosine * h_psi + turn * h_q
        n_im = cosine * h_im + turn * halo[2, k].astype(F32)
        sources[k * BLK : (k + 1) * BLK, :] = ((n_im - energy_next * n_psi) * inverse).astype(BF16)
    unmix(channels(0, CHAN))
    q, t, im = vec_q[...], vec_t[...], vec_im[...]
    sum_start(2, [(q, q), (q, im), (q, t)])
    totals = sum_finish(2)
    kappa = kappa_of(scalar(totals, 0))
    coupling = kappa * scalar(totals, 1)
    curvature = kappa * kappa * scalar(totals, 2)
    cosine, sine, lowest = rotation(energy_next, coupling, curvature)
    psi_ref[0] = cosine * start_buf[...] + (sine * kappa) * vec_q[...]
    energy_ref[...] = jnp.broadcast_to(lowest, (1, 128))

    await_rows(near_buf.at[0], NEAR, near_send.at[0])
    await_rows(near_buf.at[1], ACROSS, near_send.at[1])
    for k in range(3):
        await_rows(exchange.at[k], EVERY, red_send.at[k])
    for copies in [env_copies, start_halo] + halos:
        for copy in copies:
            copy.wait_send()


def body(wavefunction, environments, mpo_terms, sector_dims, channel_charges):
    rows = environments.reshape(2, CHAN, PAIRS, 128).transpose(1, 2, 0, 3).reshape(CHAN * PAIRS * 2, 128)
    terms = mpo_terms.transpose(1, 2, 0)
    vmem = pl.BlockSpec(memory_space=pltpu.VMEM)
    hbm = pl.BlockSpec(memory_space=pltpu.HBM)
    psi, energy = pl.pallas_call(
        kernel,
        out_shape=(
            pltpu.VMEM((1, BLK, WIDTH), F32),
            pltpu.VMEM((1, 128), F32),
        ),
        in_specs=[hbm] * 5,
        out_specs=(vmem, vmem),
        scratch_shapes=[
            pltpu.VMEM((1, BLK, WIDTH), F32),
            pltpu.VMEM((PH, PH, CHAN), BF16),
            pltpu.SMEM((1, 2), jnp.int32),
            pltpu.SMEM((CHAN,), jnp.int32),
            pltpu.VMEM((2 * CHAN * PAIRS, 128), BF16),
            pltpu.VMEM((2 * CHAN * PAIRS, 128), F32),
            pltpu.VMEM((2, CHAN * PAIRS, 128), BF16),
            pltpu.VMEM((CHAN * PAIRS, 128), BF16),
            pltpu.VMEM((CHAN * BLK, 3 * BLK), BF16),
            pltpu.VMEM((CHAN, 256, 256), BF16),
            pltpu.VMEM((CHAN, 256, 256), BF16),
            pltpu.VMEM((256, 256), F32),
            pltpu.VMEM((3 * BLK, WIDTH), BF16),
            pltpu.VMEM((3, 3, BLK, WIDTH), BF16),
            pltpu.VMEM((BLK, 128), F32),
            pltpu.VMEM((PH // 2, BLK, 128), F32),
            pltpu.VMEM((BLK, WIDTH), F32),
            pltpu.VMEM((BLK, WIDTH), F32),
            pltpu.VMEM((BLK, WIDTH), F32),
            pltpu.VMEM((BLK, WIDTH), F32),
            pltpu.VMEM((2, 8, 128), F32),
            pltpu.VMEM((3, 32, 128), F32),
            pltpu.SemaphoreType.DMA((4,)),
            pltpu.SemaphoreType.DMA((len(CHUNKS),)),
            pltpu.SemaphoreType.DMA((len(CHUNKS),)),
            pltpu.SemaphoreType.DMA((len(CHUNKS),)),
            pltpu.SemaphoreType.DMA((3, 2)),
            pltpu.SemaphoreType.DMA((3, 2)),
            pltpu.SemaphoreType.DMA((2,)),
            pltpu.SemaphoreType.DMA((2,)),
            pltpu.SemaphoreType.DMA((3,)),
            pltpu.SemaphoreType.DMA((3,)),
        ],
        compiler_params=pltpu.CompilerParams(
            collective_id=0, has_side_effects=True, vmem_limit_bytes=56 * 2**20
        ),
    )(wavefunction, rows, terms, sector_dims, channel_charges)
    return psi, energy[0, :1]


def solution(mesh):
    return jax.shard_map(
        body,
        mesh=mesh,
        in_specs=(
            P(("section", "inner"), None, None),
            P(("section", "inner"), None, None),
            P(),
            P(("section", "inner"), None),
            P(),
        ),
        out_specs=(P(("section", "inner"), None, None), P("section")),
        check_vma=False,
    )
```

```python
import functools

import jax
import jax.numpy as jnp
from jax import lax
from jax.experimental import pallas as pl
from jax.experimental.pallas import tpu as pltpu
from jax.sharding import PartitionSpec as P

MESH = pl.DeviceIdType.MESH
F32 = jnp.float32
BF16 = jnp.bfloat16

ITERS = 2
EPSILON = 1e-06
BLK = 64
CHAN = 34
PH = 16
WIDTH = PH * BLK
PAIRS = BLK // 2

NEAR = tuple((0, d) for d in range(8))
ACROSS = ((0, 0), (0, 8), (1, 0), (1, 8))
EVERY = tuple((h, d) for h in (0, 1) for d in range(16))


def distance(peer):
    h, d = peer
    return h + (d & 8) // 8 + (2 if d & 6 == 4 else 1 if d & 6 else 0)


CHUNKS = ((0, 12), (12, 24), (24, CHAN))
GROUP = 4


def flipped(index, bits):
    for bit in (1, 2, 4, 8):
        if bits & bit:
            index = index + bit * (1 - 2 * ((index // bit) % 2))
    return index


def low_half(rows):
    return lax.broadcasted_iota(jnp.int32, (rows, 128), 1) < BLK


def interchange(a, b, low):
    turned_a = pltpu.roll(a, BLK, 1)
    turned_b = pltpu.roll(b, BLK, 1)
    return jnp.where(low, a, turned_b), jnp.where(low, turned_a, b)


def to_mixed(field):
    low = low_half(16)
    rows = []
    for j in range(PH // 2):
        even, odd = [], []
        for p in range(2):
            a = field[32 * p : 32 * p + 16, 128 * j : 128 * j + 128]
            b = field[32 * p + 16 : 32 * p + 32, 128 * j : 128 * j + 128]
            first, second = interchange(a, b, low)
            even.append(first)
            odd.append(second)
        rows.append(jnp.concatenate(even, axis=1))
        rows.append(jnp.concatenate(odd, axis=1))
    return jnp.concatenate(rows, axis=0)


def kernel(
    wave_hbm, env_ref, mpo_hbm, dims_hbm, charge_hbm, psi_ref, energy_ref,
    wave_ref, mpo_ref, dims_ref, charge_ref, env_buf, wide, raw, outgoing, lsel, rsel, wsel, image, sources,
    halo, mask, columns, start_buf, im_buf, vec_im, vec_q, vec_t, near_buf, exchange,
    small_load, env_load, env_send, env_recv, halo_send, halo_recv, near_send, near_recv, red_send, red_recv,
):
    section, inner = lax.axis_index("section"), lax.axis_index("inner")
    n_inner = lax.axis_size("inner")
    parity = section % 2
    even = parity == 0
    entries = 2.0 * n_inner * BLK * WIDTH

    def at(h, d):
        return (flipped(section, h), flipped(inner, d))

    above = (section, (inner + 1) % n_inner)
    below = (section, (inner + n_inner - 1) % n_inner)
    partner = at(1, 0)

    peers = [partner, above, below] + [at(h, d) for h, d in NEAR[1:] + ACROSS[1:2] + ACROSS[3:]]
    barrier = pltpu.get_barrier_semaphore()
    for peer in peers:
        pl.semaphore_signal(barrier, inc=1, device_id=peer, device_id_type=MESH)

    small = [
        pltpu.make_async_copy(source, target, small_load.at[k])
        for k, (source, target) in enumerate(
            ((dims_hbm, dims_ref), (wave_hbm, wave_ref), (mpo_hbm, mpo_ref), (charge_hbm, charge_ref))
        )
    ]
    small[0].start()
    small[1].start()

    def env_rows(k, factor):
        first, last = CHUNKS[k]
        return pl.ds(first * PAIRS * factor, (last - first) * PAIRS * factor)

    loads = [
        pltpu.make_async_copy(env_ref.at[env_rows(k, 2)], env_buf.at[env_rows(k, 2)], env_load.at[k])
        for k in range(len(CHUNKS))
    ]
    for load in loads + small[2:]:
        load.start()

    row8 = lax.broadcasted_iota(jnp.int32, (8, 128), 0)
    lane8 = lax.broadcasted_iota(jnp.int32, (8, 128), 1)

    def dots(pairs):
        packed = jnp.zeros((8, 128), F32)
        for k, (x, y) in enumerate(pairs):
            prod = x * y
            tiles = [
                prod[8 * i : 8 * i + 8, 128 * j : 128 * j + 128] for i in range(BLK // 8) for j in range(WIDTH // 128)
            ]
            while len(tiles) > 1:
                tiles = [tiles[2 * n] + tiles[2 * n + 1] for n in range(len(tiles) // 2)]
            tile = tiles[0] + pltpu.roll(tiles[0], 64, 1)
            tile = tile + pltpu.roll(tile, 32, 1)
            packed = jnp.where(lane8 // 32 == k, tile, packed)
        return jnp.sum(packed, axis=0, keepdims=True)

    def send_row(buf, group, value, send, recv):
        buf[0:1, :] = value
        for h, d in sorted(group[1:], key=distance, reverse=True):
            j = group.index((h, d))
            pltpu.make_async_remote_copy(
                src_ref=buf.at[pl.ds(0, 1)],
                dst_ref=buf.at[pl.ds(j, 1)],
                send_sem=send,
                recv_sem=recv,
                device_id=at(h, d),
                device_id_type=MESH,
            ).start()

    def await_rows(buf, group, sem):
        rows = buf.at[pl.ds(1, len(group) - 1)]
        pltpu.make_async_copy(rows, rows, sem).wait()

    def total_rows(tile):
        for step in (4, 2, 1):
            tile = tile + pltpu.roll(tile, step, 0)
        return tile

    def scalars(tile):
        return jnp.sum(jnp.where(lane8 // 32 == row8, tile, 0.0), axis=1, keepdims=True) * (1.0 / entries)

    def sum_start(k, row):
        send_row(exchange.at[k], EVERY, row, red_send.at[k], red_recv.at[k])

    def sum_finish(k):
        await_rows(exchange.at[k], EVERY, red_recv.at[k])
        part = [exchange[k, 8 * n : 8 * n + 8, :] for n in range(4)]
        return scalars(total_rows((part[0] + part[1]) + (part[2] + part[3])))

    def halo_copies(k):
        return [
            pltpu.make_async_remote_copy(
                src_ref=halo.at[k, 1],
                dst_ref=halo.at[k, 2 * side],
                send_sem=halo_send.at[k, side],
                recv_sem=halo_recv.at[k, side],
                device_id=target,
                device_id_type=MESH,
            )
            for side, target in ((0, above), (1, below))
        ]

    def channels(first, last, midway=None):
        groups = [(a, min(a + GROUP, last)) for a in range(first, last, GROUP)]

        def left(group):
            a, b = group
            out = jnp.dot(lsel[a * BLK : b * BLK, :], sources[...], preferred_element_type=F32).astype(BF16)
            return [to_mixed(out[k * BLK : (k + 1) * BLK]) for k in range(b - a)]

        total = None
        ready = left(groups[0])
        for n, (a, b) in enumerate(groups):
            now = ready
            if n + 1 < len(groups):
                ready = left(groups[n + 1])
            if midway is not None and n == len(groups) // 2:
                midway()
            mixed = [
                jnp.dot(wsel[a + k], now[k], preferred_element_type=F32).astype(BF16) for k in range(b - a)
            ]
            right = rsel[a:b].reshape((b - a) * 256, 256)
            part = jnp.dot(jnp.concatenate(mixed, axis=1), right, preferred_element_type=F32)
            total = part if total is None else total + part
        return total

    def unmix(total):
        low = low_half(16)
        for j in range(PH // 2):
            for p in range(2):
                a = total[32 * j : 32 * j + 16, 128 * p : 128 * p + 128]
                b = total[32 * j + 16 : 32 * j + 32, 128 * p : 128 * p + 128]
                upper, lower = interchange(a, b, low)
                columns[j, pl.ds(p, 16, stride=2), :] = upper
                columns[j, pl.ds(32 + p, 16, stride=2), :] = lower
        for j in range(PH // 2):
            vec_t[:, 128 * j : 128 * j + 128] = columns[j] * mask[...]

    small[0].wait()
    small[1].wait()
    row = lax.broadcasted_iota(jnp.int32, (BLK, 128), 0)
    lane = lax.broadcasted_iota(jnp.int32, (BLK, 128), 1)
    live = (row < dims_ref[0, 0]) & (lane % BLK < dims_ref[0, 1])
    mask[...] = jnp.where(live, 1.0, 0.0).astype(F32)
    start = wave_ref[0] * jnp.concatenate([mask[...]] * (WIDTH // 128), axis=1)
    start_buf[...] = start
    halo[0, 1] = start.astype(BF16)
    norm_row = dots([(start, start)])

    for k in range(len(CHUNKS)):
        loads[k].wait()
        wide[env_rows(k, 2), :] = env_buf[env_rows(k, 2), :].astype(F32)
        first, last = CHUNKS[k]
        count = (last - first) * PAIRS
        upper = wide[pl.ds(first * PAIRS * 2, count, stride=2), :]
        lower = wide[pl.ds(first * PAIRS * 2 + 1, count, stride=2), :]
        raw[parity, env_rows(k, 1), :] = jnp.where(even, upper, lower).astype(BF16)
        outgoing[env_rows(k, 1), :] = jnp.where(even, lower, upper).astype(BF16)

    pl.semaphore_wait(barrier, len(peers))
    env_copies = [
        pltpu.make_async_remote_copy(
            src_ref=outgoing.at[env_rows(k, 1)],
            dst_ref=raw.at[parity, env_rows(k, 1)],
            send_sem=env_send.at[k],
            recv_sem=env_recv.at[k],
            device_id=partner,
            device_id_type=MESH,
        )
        for k in range(len(CHUNKS))
    ]
    start_halo = halo_copies(0)
    env_copies[0].start()
    for copy in start_halo:
        copy.start()
    for copy in env_copies[1:]:
        copy.start()
    send_row(near_buf.at[0], NEAR, norm_row, near_send.at[0], near_recv.at[0])

    def iota(shape, axis):
        return lax.broadcasted_iota(jnp.int32, shape, axis)

    small[2].wait()
    small[3].wait()
    flat = mpo_ref[...].reshape(PH * PH, CHAN)
    unit_rows = (iota((CHAN, CHAN), 0) == iota((CHAN, CHAN), 1)).astype(BF16)
    by_channel = lax.dot_general(unit_rows, flat, (((1,), (1,)), ((), ())), preferred_element_type=F32)
    keep_t = iota((PH, 256), 1) % 16 == iota((PH, 256), 0)
    picked = jnp.concatenate(
        [jnp.where(keep_t, jnp.broadcast_to(by_channel[a : a + 1, :], (PH, 256)), 0.0) for a in range(CHAN)], axis=0
    ).astype(BF16)
    widen = (iota((256, 256), 0) // 16 == iota((256, 256), 1) // 16).astype(BF16)
    terms = jnp.dot(picked, widen, preferred_element_type=F32).astype(BF16)
    spread_rows = (iota((256, PH), 0) // 16 == iota((256, PH), 1)).astype(BF16)
    same = iota((256, 256), 0) % 16 == iota((256, 256), 1) % 16
    for a in range(CHAN):
        both = jnp.dot(spread_rows, terms[a * PH : (a + 1) * PH], preferred_element_type=F32)
        wsel[a] = jnp.where(same, both, 0.0).astype(BF16)

    low32 = low_half(32)
    low64 = low_half(64)

    def doubled(slot, a):
        x = raw[slot, a * PAIRS : (a + 1) * PAIRS, :]
        turned = pltpu.roll(x, BLK, 1)
        return jnp.where(low32, x, turned), jnp.where(low32, turned, x)

    def place_left(first, last):
        for a in range(first, last):
            charge = charge_ref[a]
            here = jnp.where(low32, -1, 0) == charge
            there = jnp.logical_and(low32, charge == 1)
            for half, value in enumerate(doubled(0, a)):
                rows = slice(a * BLK + half * PAIRS, a * BLK + (half + 1) * PAIRS)
                none = jnp.zeros_like(value)
                lsel[rows, 0:128] = jnp.where(here, value, none)
                lsel[rows, 128:192] = jnp.where(there, value, none)[:, :BLK]

    def place_right(first, last):
        none = jnp.zeros((BLK, 128), BF16)
        zero = jnp.zeros((2 * BLK, 128), BF16)
        for a in range(first, last):
            upper, lower = doubled(1, a)
            wide[pl.ds(a * BLK, PAIRS, stride=2), :] = upper.astype(F32)
            wide[pl.ds(a * BLK + 1, PAIRS, stride=2), :] = lower.astype(F32)
            both = wide[a * BLK : (a + 1) * BLK, :].astype(BF16)
            block = jnp.concatenate([jnp.where(low64, both, none), jnp.where(low64, none, both)], axis=0)
            rsel[a, 0:128, 0:128] = block
            rsel[a, 128:256, 128:256] = block
            rsel[a, 0:128, 128:256] = zero
            rsel[a, 128:256, 0:128] = zero

    @pl.when(even)
    def _():
        place_left(0, CHAN)

    @pl.when(jnp.logical_not(even))
    def _():
        place_right(0, CHAN)

    await_rows(near_buf.at[0], NEAR, near_recv.at[0])
    norm_row = total_rows(near_buf[0])[0:1, :]
    send_row(near_buf.at[1], ACROSS, norm_row, near_send.at[1], near_recv.at[1])

    for copy in start_halo:
        copy.wait_recv()
    for k in range(3):
        sources[k * BLK : (k + 1) * BLK, :] = halo[0, k]
    total = None
    for k, (first, last) in enumerate(CHUNKS):
        arrived = raw.at[1 - parity, env_rows(k, 1)]
        pltpu.make_async_copy(arrived, arrived, env_recv.at[k]).wait()

        @pl.when(even)
        def _():
            place_right(first, last)

        @pl.when(jnp.logical_not(even))
        def _():
            place_left(first, last)

        if k:
            image[...] += channels(first, last)
        else:
            image[...] = channels(first, last)

    await_rows(near_buf.at[1], ACROSS, near_recv.at[1])
    part = [near_buf[1, k : k + 1, :] for k in range(4)]
    norm_row = (part[0] + part[1]) + (part[2] + part[3])
    norm = jnp.sum(jnp.where(lane8[0:1] < 32, norm_row, 0.0), axis=1, keepdims=True) * (1.0 / entries)
    scale = 1.0 / jnp.sqrt(norm + EPSILON)
    unmix(image[...])
    im = vec_t[...] * scale
    vec_im[...] = im
    halo[1, 1] = im.astype(BF16)
    halos = [halo_copies(1), halo_copies(2)]
    for copy in halos[0]:
        copy.start()
    psi = start_buf[...] * scale
    start_buf[...] = psi

    def scalar(total, k):
        return total[k : k + 1, :]

    def rotation(energy, coupling, curvature):
        x = 0.5 * (curvature - energy)
        size = jnp.maximum(jnp.abs(x), jnp.abs(coupling))
        safe = jnp.where(size > 0.0, size, 1.0)
        xs, ys = x / safe, -coupling / safe
        radius = jnp.sqrt(xs * xs + ys * ys)
        radius = jnp.where(size > 0.0, radius, 1.0)
        cos2 = jnp.where(size > 0.0, xs / radius, 1.0)
        sin2 = ys / radius
        big = jnp.sqrt(0.5 + 0.5 * jnp.abs(cos2))
        small = 0.5 * sin2 / big
        sign = jnp.where(coupling < 0.0, 1.0, -1.0)
        cosine = jnp.where(cos2 >= 0.0, big, jnp.abs(small))
        sine = jnp.where(cos2 >= 0.0, small, sign * big)
        lowest = 0.5 * (energy + curvature) - jnp.sqrt(x * x + coupling * coupling)
        return cosine, sine, lowest

    def kappa_of(square):
        return unit / jnp.sqrt(unit * unit * square + EPSILON)

    def own(row):
        return scalars(jnp.broadcast_to(row, (8, 128)))

    share = 1.0 / (2 * n_inner)
    row_sums = dots([(psi, im), (im, im), (psi, psi)])
    sum_start(0, row_sums)
    local = own(row_sums)
    weight = jnp.maximum(scalar(local, 2), 0.5 * share)
    quotient = scalar(local, 0) / weight
    sources[BLK : 2 * BLK, :] = (vec_im[...] - quotient * start_buf[...]).astype(BF16)
    scaled = quotient * scale
    for copy in halos[0]:
        copy.wait_recv()
    for k in (0, 2):
        field = halo[1, k].astype(F32) - scaled * halo[0, k].astype(F32)
        sources[k * BLK : (k + 1) * BLK, :] = field.astype(BF16)
    sums = {}

    def read_first():
        sums[0] = sum_finish(0)

    unmix(channels(0, CHAN, read_first))
    energy_now = scalar(sums[0], 0)
    square = scalar(sums[0], 1)
    unit = jnp.sqrt(square + EPSILON)
    inverse = 1.0 / unit
    t = (vec_t[...] + (quotient - energy_now) * vec_im[...]) * inverse
    vec_t[...] = t
    halo[2, 1] = t.astype(BF16)
    for copy in halos[1]:
        copy.start()
    q = (vec_im[...] - energy_now * start_buf[...]) * inverse
    vec_q[...] = q

    row_sums = dots([(q, q), (q, vec_im[...]), (q, vec_t[...]), (start_buf[...], vec_t[...])])
    sum_start(1, row_sums)
    local = own(row_sums)
    rest = square + energy_now * (energy_now * scalar(sums[0], 2) - 2.0 * energy_now)
    floor = 0.5 * share * jnp.maximum(rest * inverse * inverse, 1e-6)
    along_q = scalar(local, 2) / jnp.maximum(scalar(local, 0), floor)
    along_psi = scalar(local, 3) / weight
    sources[BLK : 2 * BLK, :] = (vec_t[...] - along_q * vec_q[...] - along_psi * start_buf[...]).astype(BF16)
    of_im = along_q * inverse
    of_start = (along_psi - of_im * energy_now) * scale
    for copy in halos[1]:
        copy.wait_recv()
    for k in (0, 2):
        field = halo[2, k].astype(F32) - of_im * halo[1, k].astype(F32) - of_start * halo[0, k].astype(F32)
        sources[k * BLK : (k + 1) * BLK, :] = field.astype(BF16)

    def read_second():
        sums[1] = sum_finish(1)

    turned_t = channels(0, CHAN, read_second)
    totals = sums[1]
    kappa = kappa_of(scalar(totals, 0))
    coupling = kappa * scalar(totals, 1)
    curvature = kappa * kappa * scalar(totals, 2)
    mirrored = kappa * scalar(totals, 3)
    cosine, sine, _ = rotation(energy_now, coupling, curvature)
    energy_next = (
        cosine * cosine * energy_now + cosine * sine * (coupling + mirrored) + sine * sine * curvature
    )
    turn = sine * kappa
    psi = cosine * start_buf[...] + turn * vec_q[...]
    im = cosine * vec_im[...] + turn * vec_t[...]
    known = (cosine * unit + turn * along_q) * vec_t[...] + (cosine * energy_now + turn * along_psi) * vec_im[...]
    start_buf[...] = psi
    q = (im - energy_next * psi) * inverse
    vec_q[...] = q
    vec_im[...] = known - energy_next * im
    im_buf[...] = im
    unmix(turned_t)
    t = (vec_im[...] + turn * vec_t[...]) * inverse
    sum_start(2, dots([(vec_q[...], vec_q[...]), (vec_q[...], im_buf[...]), (vec_q[...], t)]))
    totals = sum_finish(2)
    kappa = kappa_of(scalar(totals, 0))
    coupling = kappa * scalar(totals, 1)
    curvature = kappa * kappa * scalar(totals, 2)
    cosine, sine, lowest = rotation(energy_next, coupling, curvature)
    psi_ref[0] = cosine * start_buf[...] + (sine * kappa) * vec_q[...]
    energy_ref[...] = jnp.broadcast_to(lowest, (1, 128))

    await_rows(near_buf.at[0], NEAR, near_send.at[0])
    await_rows(near_buf.at[1], ACROSS, near_send.at[1])
    for k in range(3):
        await_rows(exchange.at[k], EVERY, red_send.at[k])
    for copies in [env_copies, start_halo] + halos:
        for copy in copies:
            copy.wait_send()


def body(wavefunction, environments, mpo_terms, sector_dims, channel_charges):
    rows = environments.reshape(2, CHAN, PAIRS, 128).transpose(1, 2, 0, 3).reshape(CHAN * PAIRS * 2, 128)
    terms = mpo_terms.transpose(1, 2, 0)
    vmem = pl.BlockSpec(memory_space=pltpu.VMEM)
    hbm = pl.BlockSpec(memory_space=pltpu.HBM)
    psi, energy = pl.pallas_call(
        kernel,
        out_shape=(
            pltpu.VMEM((1, BLK, WIDTH), F32),
            pltpu.VMEM((1, 128), F32),
        ),
        in_specs=[hbm] * 5,
        out_specs=(vmem, vmem),
        scratch_shapes=[
            pltpu.VMEM((1, BLK, WIDTH), F32),
            pltpu.VMEM((PH, PH, CHAN), BF16),
            pltpu.SMEM((1, 2), jnp.int32),
            pltpu.SMEM((CHAN,), jnp.int32),
            pltpu.VMEM((2 * CHAN * PAIRS, 128), BF16),
            pltpu.VMEM((2 * CHAN * PAIRS, 128), F32),
            pltpu.VMEM((2, CHAN * PAIRS, 128), BF16),
            pltpu.VMEM((CHAN * PAIRS, 128), BF16),
            pltpu.VMEM((CHAN * BLK, 3 * BLK), BF16),
            pltpu.VMEM((CHAN, 256, 256), BF16),
            pltpu.VMEM((CHAN, 256, 256), BF16),
            pltpu.VMEM((256, 256), F32),
            pltpu.VMEM((3 * BLK, WIDTH), BF16),
            pltpu.VMEM((3, 3, BLK, WIDTH), BF16),
            pltpu.VMEM((BLK, 128), F32),
            pltpu.VMEM((PH // 2, BLK, 128), F32),
            pltpu.VMEM((BLK, WIDTH), F32),
            pltpu.VMEM((BLK, WIDTH), F32),
            pltpu.VMEM((BLK, WIDTH), F32),
            pltpu.VMEM((BLK, WIDTH), F32),
            pltpu.VMEM((BLK, WIDTH), F32),
            pltpu.VMEM((2, 8, 128), F32),
            pltpu.VMEM((3, 32, 128), F32),
            pltpu.SemaphoreType.DMA((4,)),
            pltpu.SemaphoreType.DMA((len(CHUNKS),)),
            pltpu.SemaphoreType.DMA((len(CHUNKS),)),
            pltpu.SemaphoreType.DMA((len(CHUNKS),)),
            pltpu.SemaphoreType.DMA((3, 2)),
            pltpu.SemaphoreType.DMA((3, 2)),
            pltpu.SemaphoreType.DMA((2,)),
            pltpu.SemaphoreType.DMA((2,)),
            pltpu.SemaphoreType.DMA((3,)),
            pltpu.SemaphoreType.DMA((3,)),
        ],
        compiler_params=pltpu.CompilerParams(
            collective_id=0, has_side_effects=True, vmem_limit_bytes=56 * 2**20
        ),
    )(wavefunction, rows, terms, sector_dims, channel_charges)
    return psi, energy[0, :1]


def solution(mesh):
    return jax.shard_map(
        body,
        mesh=mesh,
        in_specs=(
            P(("section", "inner"), None, None),
            P(("section", "inner"), None, None),
            P(),
            P(("section", "inner"), None),
            P(),
        ),
        out_specs=(P(("section", "inner"), None, None), P("section")),
        check_vma=False,
    )
```

```python
import functools

import jax
import jax.numpy as jnp
from jax import lax
from jax.experimental import pallas as pl
from jax.experimental.pallas import tpu as pltpu
from jax.sharding import PartitionSpec as P

MESH = pl.DeviceIdType.MESH
F32 = jnp.float32
BF16 = jnp.bfloat16

ITERS = 2
EPSILON = 1e-06
BLK = 64
CHAN = 34
PH = 16
WIDTH = PH * BLK
PAIRS = BLK // 2

NEAR = tuple((0, d) for d in range(8))
ACROSS = ((0, 0), (0, 8), (1, 0), (1, 8))
EVERY = tuple((h, d) for h in (0, 1) for d in range(16))


def distance(peer):
    h, d = peer
    return h + (d & 8) // 8 + (2 if d & 6 == 4 else 1 if d & 6 else 0)


CHUNKS = ((0, 18), (18, CHAN))
GROUP = 4


def flipped(index, bits):
    for bit in (1, 2, 4, 8):
        if bits & bit:
            index = index + bit * (1 - 2 * ((index // bit) % 2))
    return index


def low_half(rows):
    return lax.broadcasted_iota(jnp.int32, (rows, 128), 1) < BLK


def interchange(a, b, low):
    turned_a = pltpu.roll(a, BLK, 1)
    turned_b = pltpu.roll(b, BLK, 1)
    return jnp.where(low, a, turned_b), jnp.where(low, turned_a, b)


def to_mixed(field):
    low = low_half(16)
    rows = []
    for j in range(PH // 2):
        even, odd = [], []
        for p in range(2):
            a = field[32 * p : 32 * p + 16, 128 * j : 128 * j + 128]
            b = field[32 * p + 16 : 32 * p + 32, 128 * j : 128 * j + 128]
            first, second = interchange(a, b, low)
            even.append(first)
            odd.append(second)
        rows.append(jnp.concatenate(even, axis=1))
        rows.append(jnp.concatenate(odd, axis=1))
    return jnp.concatenate(rows, axis=0)


def kernel(
    wave_hbm, env_ref, mpo_hbm, dims_hbm, charge_hbm, psi_ref, energy_ref,
    wave_ref, mpo_ref, dims_ref, charge_ref, env_buf, wide, woven, raw, outgoing, lsel, rsel, wsel, image, sources,
    halo, mask, start_buf, im_buf, vec_im, vec_q, vec_t, near_buf, exchange,
    small_load, env_load, env_send, env_recv, halo_send, halo_recv, near_send, near_recv, red_send, red_recv,
):
    section, inner = lax.axis_index("section"), lax.axis_index("inner")
    n_inner = lax.axis_size("inner")
    parity = section % 2
    even = parity == 0
    entries = 2.0 * n_inner * BLK * WIDTH

    sections = [flipped(section, h) for h in (0, 1)]
    inners = [flipped(inner, d) for d in range(16)]

    def at(h, d):
        return (sections[h], inners[d])

    above = (section, (inner + 1) % n_inner)
    below = (section, (inner + n_inner - 1) % n_inner)
    partner = at(1, 0)

    peers = [partner, above, below] + [at(h, d) for h, d in NEAR[1:] + ACROSS[1:2] + ACROSS[3:]]
    barrier = pltpu.get_barrier_semaphore()
    for peer in peers:
        pl.semaphore_signal(barrier, inc=1, device_id=peer, device_id_type=MESH)

    small = [
        pltpu.make_async_copy(source, target, small_load.at[k])
        for k, (source, target) in enumerate(
            ((dims_hbm, dims_ref), (wave_hbm, wave_ref), (mpo_hbm, mpo_ref), (charge_hbm, charge_ref))
        )
    ]
    small[0].start()
    small[1].start()

    def env_rows(k, factor):
        first, last = CHUNKS[k]
        return pl.ds(first * PAIRS * factor, (last - first) * PAIRS * factor)

    loads = [
        pltpu.make_async_copy(env_ref.at[env_rows(k, 2)], env_buf.at[env_rows(k, 2)], env_load.at[k])
        for k in range(len(CHUNKS))
    ]
    for load in loads + small[2:]:
        load.start()

    row8 = lax.broadcasted_iota(jnp.int32, (8, 128), 0)
    lane8 = lax.broadcasted_iota(jnp.int32, (8, 128), 1)

    def partial(x, y):
        prod = x * y
        tiles = [
            prod[8 * i : 8 * i + 8, 128 * j : 128 * j + 128] for i in range(BLK // 8) for j in range(WIDTH // 128)
        ]
        while len(tiles) > 1:
            tiles = [tiles[2 * n] + tiles[2 * n + 1] for n in range(len(tiles) // 2)]
        tile = tiles[0] + pltpu.roll(tiles[0], 64, 1)
        return tile + pltpu.roll(tile, 32, 1)

    def packed(tiles):
        total = jnp.zeros((8, 128), F32)
        for k, tile in enumerate(tiles):
            total = jnp.where(lane8 // 32 == k, tile, total)
        return jnp.sum(total, axis=0, keepdims=True)

    def dots(pairs):
        return packed([partial(x, y) for x, y in pairs])

    def send_row(buf, group, value, send, recv):
        buf[0:1, :] = value
        for h, d in sorted(group[1:], key=distance, reverse=True):
            j = group.index((h, d))
            pltpu.make_async_remote_copy(
                src_ref=buf.at[pl.ds(0, 1)],
                dst_ref=buf.at[pl.ds(j, 1)],
                send_sem=send,
                recv_sem=recv,
                device_id=at(h, d),
                device_id_type=MESH,
            ).start()

    def await_rows(buf, group, sem):
        rows = buf.at[pl.ds(1, len(group) - 1)]
        pltpu.make_async_copy(rows, rows, sem).wait()

    def total_rows(tile):
        for step in (4, 2, 1):
            tile = tile + pltpu.roll(tile, step, 0)
        return tile

    def scalars(tile):
        return jnp.sum(jnp.where(lane8 // 32 == row8, tile, 0.0), axis=1, keepdims=True) * (1.0 / entries)

    def sum_start(k, row):
        send_row(exchange.at[k], EVERY, row, red_send.at[k], red_recv.at[k])

    def sum_finish(k):
        await_rows(exchange.at[k], EVERY, red_recv.at[k])
        part = [exchange[k, 8 * n : 8 * n + 8, :] for n in range(4)]
        return scalars(total_rows((part[0] + part[1]) + (part[2] + part[3])))

    def halo_copies(k):
        return [
            pltpu.make_async_remote_copy(
                src_ref=halo.at[k, 1],
                dst_ref=halo.at[k, 2 * side],
                send_sem=halo_send.at[k, side],
                recv_sem=halo_recv.at[k, side],
                device_id=target,
                device_id_type=MESH,
            )
            for side, target in ((0, above), (1, below))
        ]

    def channels(first, last, midway=None, size=GROUP):
        groups = [(a, min(a + size, last)) for a in range(first, last, size)]

        def left(group):
            a, b = group
            out = jnp.dot(lsel[a * BLK : b * BLK, :], sources[...], preferred_element_type=F32).astype(BF16)
            return [to_mixed(out[k * BLK : (k + 1) * BLK]) for k in range(b - a)]

        total = None
        ready = left(groups[0])
        for n, (a, b) in enumerate(groups):
            now = ready
            if n + 1 < len(groups):
                ready = left(groups[n + 1])
            if midway is not None and n == len(groups) // 2:
                midway()
            mixed = [
                jnp.dot(wsel[a + k], now[k], preferred_element_type=F32).astype(BF16) for k in range(b - a)
            ]
            right = rsel[a:b].reshape((b - a) * 256, 256)
            part = jnp.dot(jnp.concatenate(mixed, axis=1), right, preferred_element_type=F32)
            total = part if total is None else total + part
        return total

    def unmix(total):
        low = low_half(16)
        for j in range(PH // 2):
            lanes = slice(128 * j, 128 * j + 128)
            for p in range(2):
                a = total[32 * j : 32 * j + 16, 128 * p : 128 * p + 128]
                b = total[32 * j + 16 : 32 * j + 32, 128 * p : 128 * p + 128]
                for half, value in enumerate(interchange(a, b, low)):
                    rows = slice(32 * p + 16 * half, 32 * p + 16 * half + 16)
                    vec_t[rows, lanes] = value * mask[rows, :]

    small[0].wait()
    small[1].wait()
    row = lax.broadcasted_iota(jnp.int32, (BLK, 128), 0)
    lane = lax.broadcasted_iota(jnp.int32, (BLK, 128), 1)
    live = (row < dims_ref[0, 0]) & (lane % BLK < dims_ref[0, 1])
    mask[...] = jnp.where(live, 1.0, 0.0).astype(F32)
    start = wave_ref[0] * jnp.concatenate([mask[...]] * (WIDTH // 128), axis=1)
    start_buf[...] = start
    halo[0, 1] = start.astype(BF16)
    norm_row = dots([(start, start)])

    for k in range(len(CHUNKS)):
        loads[k].wait()
        wide[env_rows(k, 2), :] = env_buf[env_rows(k, 2), :].astype(F32)
        first, last = CHUNKS[k]
        count = (last - first) * PAIRS
        upper = wide[pl.ds(first * PAIRS * 2, count, stride=2), :]
        lower = wide[pl.ds(first * PAIRS * 2 + 1, count, stride=2), :]
        for side, value in enumerate((jnp.where(even, upper, lower), jnp.where(even, lower, upper))):
            for a in range(last - first):
                here = (first + a) * PAIRS
                x, y = value[a * PAIRS : a * PAIRS + 16], value[a * PAIRS + 16 : (a + 1) * PAIRS]
                evens, odds = interchange(x, y, low_half(16))
                woven[side, pl.ds(here, 16, stride=2), :] = evens
                woven[side, pl.ds(here + 1, 16, stride=2), :] = odds
        raw[parity, env_rows(k, 1), :] = woven[0, env_rows(k, 1), :].astype(BF16)
        outgoing[env_rows(k, 1), :] = woven[1, env_rows(k, 1), :].astype(BF16)

    pl.semaphore_wait(barrier, len(peers))
    env_copies = [
        pltpu.make_async_remote_copy(
            src_ref=outgoing.at[env_rows(k, 1)],
            dst_ref=raw.at[parity, env_rows(k, 1)],
            send_sem=env_send.at[k],
            recv_sem=env_recv.at[k],
            device_id=partner,
            device_id_type=MESH,
        )
        for k in range(len(CHUNKS))
    ]
    start_halo = halo_copies(0)
    env_copies[0].start()
    for copy in start_halo:
        copy.start()
    for copy in env_copies[1:]:
        copy.start()
    send_row(near_buf.at[0], NEAR, norm_row, near_send.at[0], near_recv.at[0])

    zero = jnp.zeros((2 * BLK, 128), BF16)
    for a in range(CHAN):
        rsel[a, 0:128, 128:256] = zero
        rsel[a, 128:256, 0:128] = zero

    def iota(shape, axis):
        return lax.broadcasted_iota(jnp.int32, shape, axis)

    small[2].wait()
    small[3].wait()
    flat = mpo_ref[...].reshape(PH * PH, CHAN)
    unit_rows = (iota((CHAN, CHAN), 0) == iota((CHAN, CHAN), 1)).astype(BF16)
    by_channel = lax.dot_general(unit_rows, flat, (((1,), (1,)), ((), ())), preferred_element_type=F32)
    keep_t = iota((PH, 256), 1) % 16 == iota((PH, 256), 0)
    picked = jnp.concatenate(
        [jnp.where(keep_t, jnp.broadcast_to(by_channel[a : a + 1, :], (PH, 256)), 0.0) for a in range(CHAN)], axis=0
    ).astype(BF16)
    widen = (iota((256, 256), 0) // 16 == iota((256, 256), 1) // 16).astype(BF16)
    terms = jnp.dot(picked, widen, preferred_element_type=F32).astype(BF16)
    spread_rows = (iota((256, PH), 0) // 16 == iota((256, PH), 1)).astype(BF16)
    same = iota((256, 256), 0) % 16 == iota((256, 256), 1) % 16
    for a in range(CHAN):
        both = jnp.dot(spread_rows, terms[a * PH : (a + 1) * PH], preferred_element_type=F32)
        wsel[a] = jnp.where(same, both, 0.0).astype(BF16)

    low32 = low_half(32)
    low64 = low_half(64)

    def doubled(slot, a):
        x = raw[slot, a * PAIRS : (a + 1) * PAIRS, :]
        turned = pltpu.roll(x, BLK, 1)
        return jnp.where(low32, x, turned), jnp.where(low32, turned, x)

    def place_left(first, last):
        for a in range(first, last):
            charge = charge_ref[a]
            here = jnp.where(low32, -1, 0) == charge
            there = jnp.logical_and(low32, charge == 1)
            for half, value in enumerate(doubled(0, a)):
                rows = slice(a * BLK + half * PAIRS, a * BLK + (half + 1) * PAIRS)
                none = jnp.zeros_like(value)
                lsel[rows, 0:128] = jnp.where(here, value, none)
                lsel[rows, 128:192] = jnp.where(there, value, none)[:, :BLK]

    def place_right(first, last):
        none = jnp.zeros((BLK, 128), BF16)
        for a in range(first, last):
            both = jnp.concatenate(doubled(1, a), axis=0)
            block = jnp.concatenate([jnp.where(low64, both, none), jnp.where(low64, none, both)], axis=0)
            rsel[a, 0:128, 0:128] = block
            rsel[a, 128:256, 128:256] = block

    @pl.when(even)
    def _():
        place_left(0, CHAN)

    @pl.when(jnp.logical_not(even))
    def _():
        place_right(0, CHAN)

    await_rows(near_buf.at[0], NEAR, near_recv.at[0])
    norm_row = total_rows(near_buf[0])[0:1, :]
    send_row(near_buf.at[1], ACROSS, norm_row, near_send.at[1], near_recv.at[1])

    def receive(k):
        first, last = CHUNKS[k]
        arrived = raw.at[1 - parity, env_rows(k, 1)]
        pltpu.make_async_copy(arrived, arrived, env_recv.at[k]).wait()

        @pl.when(even)
        def _():
            place_right(first, last)

        @pl.when(jnp.logical_not(even))
        def _():
            place_left(first, last)

    receive(0)
    for copy in start_halo:
        copy.wait_recv()
    for k in range(3):
        sources[k * BLK : (k + 1) * BLK, :] = halo[0, k]
    for k, (first, last) in enumerate(CHUNKS):
        if k:
            receive(k)
        if k:
            image[...] += channels(first, last)
        else:
            image[...] = channels(first, last)

    await_rows(near_buf.at[1], ACROSS, near_recv.at[1])
    part = [near_buf[1, k : k + 1, :] for k in range(4)]
    norm_row = (part[0] + part[1]) + (part[2] + part[3])
    norm = jnp.sum(jnp.where(lane8[0:1] < 32, norm_row, 0.0), axis=1, keepdims=True) * (1.0 / entries)
    scale = 1.0 / jnp.sqrt(norm + EPSILON)
    unmix(image[...])
    im = vec_t[...] * scale
    vec_im[...] = im
    halo[1, 1] = im.astype(BF16)
    halos = [halo_copies(1), halo_copies(2)]
    for copy in halos[0]:
        copy.start()
    psi = start_buf[...] * scale
    start_buf[...] = psi

    def scalar(total, k):
        return total[k : k + 1, :]

    def rotation(energy, coupling, curvature):
        x = 0.5 * (curvature - energy)
        size = jnp.maximum(jnp.abs(x), jnp.abs(coupling))
        safe = jnp.where(size > 0.0, size, 1.0)
        xs, ys = x / safe, -coupling / safe
        radius = jnp.sqrt(xs * xs + ys * ys)
        radius = jnp.where(size > 0.0, radius, 1.0)
        cos2 = jnp.where(size > 0.0, xs / radius, 1.0)
        sin2 = ys / radius
        big = jnp.sqrt(0.5 + 0.5 * jnp.abs(cos2))
        small = 0.5 * sin2 / big
        sign = jnp.where(coupling < 0.0, 1.0, -1.0)
        cosine = jnp.where(cos2 >= 0.0, big, jnp.abs(small))
        sine = jnp.where(cos2 >= 0.0, small, sign * big)
        lowest = 0.5 * (energy + curvature) - jnp.sqrt(x * x + coupling * coupling)
        return cosine, sine, lowest

    def kappa_of(unit, square):
        return unit / jnp.sqrt(unit * unit * square + EPSILON)

    def own(row):
        return scalars(jnp.broadcast_to(row, (8, 128)))

    share = 1.0 / (2 * n_inner)
    row_sums = dots([(psi, im), (im, im), (psi, psi)])
    sum_start(0, row_sums)
    local = own(row_sums)
    weight = jnp.maximum(scalar(local, 2), 0.5 * share)
    quotient = scalar(local, 0) / weight
    sources[BLK : 2 * BLK, :] = (vec_im[...] - quotient * start_buf[...]).astype(BF16)
    scaled = quotient * scale
    for copy in halos[0]:
        copy.wait_recv()
    for k in (0, 2):
        field = halo[1, k].astype(F32) - scaled * halo[0, k].astype(F32)
        sources[k * BLK : (k + 1) * BLK, :] = field.astype(BF16)
    found = {}

    def read_first():
        totals = sum_finish(0)
        energy = scalar(totals, 0)
        square = scalar(totals, 1)
        unit = jnp.sqrt(square + EPSILON)
        inverse = 1.0 / unit
        im = vec_im[...]
        q = (im - energy * start_buf[...]) * inverse
        vec_q[...] = q
        im_buf[...] = ((quotient - energy) * inverse) * im
        rest = square + energy * (energy * scalar(totals, 2) - 2.0 * energy)
        floor = 0.5 * share * jnp.maximum(rest * inverse * inverse, 1e-6)
        found[0] = energy, unit, inverse, floor, partial(q, q), partial(q, im)

    unmix(channels(0, CHAN, read_first, 5))
    energy_now, unit, inverse, floor, part_qq, part_qi = found[0]
    t = vec_t[...] * inverse + im_buf[...]
    vec_t[...] = t
    halo[2, 1] = t.astype(BF16)
    for copy in halos[1]:
        copy.start()

    t = vec_t[...]
    row_sums = packed([part_qq, part_qi, partial(vec_q[...], t), partial(start_buf[...], t)])
    sum_start(1, row_sums)
    local = own(row_sums)
    along_q = scalar(local, 2) / jnp.maximum(scalar(local, 0), floor)
    along_psi = scalar(local, 3) / weight
    sources[BLK : 2 * BLK, :] = (vec_t[...] - along_q * vec_q[...] - along_psi * start_buf[...]).astype(BF16)
    of_im = along_q * inverse
    of_start = (along_psi - of_im * energy_now) * scale
    for copy in halos[1]:
        copy.wait_recv()
    for k in (0, 2):
        field = halo[2, k].astype(F32) - of_im * halo[1, k].astype(F32) - of_start * halo[0, k].astype(F32)
        sources[k * BLK : (k + 1) * BLK, :] = field.astype(BF16)

    def read_second():
        totals = sum_finish(1)
        kappa = kappa_of(unit, scalar(totals, 0))
        coupling = kappa * scalar(totals, 1)
        curvature = kappa * kappa * scalar(totals, 2)
        mirrored = kappa * scalar(totals, 3)
        cosine, sine, _ = rotation(energy_now, coupling, curvature)
        energy = (
            cosine * cosine * energy_now + cosine * sine * (coupling + mirrored) + sine * sine * curvature
        )
        turn = sine * kappa
        im_then, t_then = vec_im[...], vec_t[...]
        psi = cosine * start_buf[...] + turn * vec_q[...]
        im = cosine * im_then + turn * t_then
        q = (im - energy * psi) * inverse
        known = (cosine * unit + turn * along_q) * t_then + (cosine * energy_now + turn * along_psi) * im_then
        start_buf[...] = psi
        vec_q[...] = q
        vec_im[...] = (known - energy * im) * inverse
        found[1] = energy, turn * inverse, partial(q, q), partial(q, im)

    unmix(channels(0, CHAN, read_second, 5))
    energy_next, factor, part_qq, part_qi = found[1]
    t = vec_t[...] * factor + vec_im[...]
    sum_start(2, packed([part_qq, part_qi, partial(vec_q[...], t)]))
    totals = sum_finish(2)
    kappa = kappa_of(unit, scalar(totals, 0))
    coupling = kappa * scalar(totals, 1)
    curvature = kappa * kappa * scalar(totals, 2)
    cosine, sine, lowest = rotation(energy_next, coupling, curvature)
    psi_ref[0] = cosine * start_buf[...] + (sine * kappa) * vec_q[...]
    energy_ref[...] = jnp.broadcast_to(lowest, (1, 128))

    await_rows(near_buf.at[0], NEAR, near_send.at[0])
    await_rows(near_buf.at[1], ACROSS, near_send.at[1])
    for k in range(3):
        await_rows(exchange.at[k], EVERY, red_send.at[k])
    for copies in [env_copies, start_halo] + halos:
        for copy in copies:
            copy.wait_send()


def body(wavefunction, environments, mpo_terms, sector_dims, channel_charges):
    rows = environments.reshape(2, CHAN, PAIRS, 128).transpose(1, 2, 0, 3).reshape(CHAN * PAIRS * 2, 128)
    terms = mpo_terms.transpose(1, 2, 0)
    vmem = pl.BlockSpec(memory_space=pltpu.VMEM)
    hbm = pl.BlockSpec(memory_space=pltpu.HBM)
    psi, energy = pl.pallas_call(
        kernel,
        out_shape=(
            pltpu.VMEM((1, BLK, WIDTH), F32),
            pltpu.VMEM((1, 128), F32),
        ),
        in_specs=[hbm] * 5,
        out_specs=(vmem, vmem),
        scratch_shapes=[
            pltpu.VMEM((1, BLK, WIDTH), F32),
            pltpu.VMEM((PH, PH, CHAN), BF16),
            pltpu.SMEM((1, 2), jnp.int32),
            pltpu.SMEM((CHAN,), jnp.int32),
            pltpu.VMEM((2 * CHAN * PAIRS, 128), BF16),
            pltpu.VMEM((2 * CHAN * PAIRS, 128), F32),
            pltpu.VMEM((2, CHAN * PAIRS, 128), F32),
            pltpu.VMEM((2, CHAN * PAIRS, 128), BF16),
            pltpu.VMEM((CHAN * PAIRS, 128), BF16),
            pltpu.VMEM((CHAN * BLK, 3 * BLK), BF16),
            pltpu.VMEM((CHAN, 256, 256), BF16),
            pltpu.VMEM((CHAN, 256, 256), BF16),
            pltpu.VMEM((256, 256), F32),
            pltpu.VMEM((3 * BLK, WIDTH), BF16),
            pltpu.VMEM((3, 3, BLK, WIDTH), BF16),
            pltpu.VMEM((BLK, 128), F32),
            pltpu.VMEM((BLK, WIDTH), F32),
            pltpu.VMEM((BLK, WIDTH), F32),
            pltpu.VMEM((BLK, WIDTH), F32),
            pltpu.VMEM((BLK, WIDTH), F32),
            pltpu.VMEM((BLK, WIDTH), F32),
            pltpu.VMEM((2, 8, 128), F32),
            pltpu.VMEM((3, 32, 128), F32),
            pltpu.SemaphoreType.DMA((4,)),
            pltpu.SemaphoreType.DMA((len(CHUNKS),)),
            pltpu.SemaphoreType.DMA((len(CHUNKS),)),
            pltpu.SemaphoreType.DMA((len(CHUNKS),)),
            pltpu.SemaphoreType.DMA((3, 2)),
            pltpu.SemaphoreType.DMA((3, 2)),
            pltpu.SemaphoreType.DMA((2,)),
            pltpu.SemaphoreType.DMA((2,)),
            pltpu.SemaphoreType.DMA((3,)),
            pltpu.SemaphoreType.DMA((3,)),
        ],
        compiler_params=pltpu.CompilerParams(
            collective_id=0, has_side_effects=True, vmem_limit_bytes=56 * 2**20
        ),
    )(wavefunction, rows, terms, sector_dims, channel_charges)
    return psi, energy[0, :1]


def solution(mesh):
    return jax.shard_map(
        body,
        mesh=mesh,
        in_specs=(
            P(("section", "inner"), None, None),
            P(("section", "inner"), None, None),
            P(),
            P(("section", "inner"), None),
            P(),
        ),
        out_specs=(P(("section", "inner"), None, None), P("section")),
        check_vma=False,
    )
```

```python
import functools

import jax
import jax.numpy as jnp
from jax import lax
from jax.experimental import pallas as pl
from jax.experimental.pallas import tpu as pltpu
from jax.sharding import PartitionSpec as P

MESH = pl.DeviceIdType.MESH
F32 = jnp.float32
BF16 = jnp.bfloat16

ITERS = 2
EPSILON = 1e-06
BLK = 64
CHAN = 34
PH = 16
WIDTH = PH * BLK
PAIRS = BLK // 2

CORES = ((0, 0), (0, 1))
RING = ((0, 0), (0, 2), (0, 4), (0, 6))
ACROSS = ((0, 0), (0, 8), (1, 0), (1, 8))
EVERY = tuple((h, d) for h in (0, 1) for d in range(16))


def distance(peer):
    h, d = peer
    return h + (d & 8) // 8 + (2 if d & 6 == 4 else 1 if d & 6 else 0)


CHUNKS = ((0, 18), (18, CHAN))
GROUP = 4


def flipped(index, bits):
    for bit in (1, 2, 4, 8):
        if bits & bit:
            index = index + bit * (1 - 2 * ((index // bit) % 2))
    return index


def low_half(rows):
    return lax.broadcasted_iota(jnp.int32, (rows, 128), 1) < BLK


def interchange(a, b, low):
    turned_a = pltpu.roll(a, BLK, 1)
    turned_b = pltpu.roll(b, BLK, 1)
    return jnp.where(low, a, turned_b), jnp.where(low, turned_a, b)


def to_mixed(field):
    low = low_half(16)
    rows = []
    for j in range(PH // 2):
        even, odd = [], []
        for p in range(2):
            a = field[32 * p : 32 * p + 16, 128 * j : 128 * j + 128]
            b = field[32 * p + 16 : 32 * p + 32, 128 * j : 128 * j + 128]
            first, second = interchange(a, b, low)
            even.append(first)
            odd.append(second)
        rows.append(jnp.concatenate(even, axis=1))
        rows.append(jnp.concatenate(odd, axis=1))
    return jnp.concatenate(rows, axis=0)


def kernel(
    wave_hbm, env_ref, mpo_hbm, dims_hbm, charge_hbm, psi_ref, energy_ref,
    wave_ref, mpo_ref, dims_ref, charge_ref, env_buf, wide, woven, raw, outgoing, lsel, rsel, wsel, image, sources,
    halo, mask, start_buf, im_buf, vec_im, vec_q, vec_t, near_buf, exchange,
    small_load, env_load, env_send, env_recv, halo_send, halo_recv, near_send, near_recv, red_send, red_recv,
):
    section, inner = lax.axis_index("section"), lax.axis_index("inner")
    n_inner = lax.axis_size("inner")
    parity = section % 2
    even = parity == 0
    entries = 2.0 * n_inner * BLK * WIDTH

    sections = [flipped(section, h) for h in (0, 1)]
    inners = [flipped(inner, d) for d in range(16)]

    def at(h, d):
        return (sections[h], inners[d])

    above = (section, (inner + 1) % n_inner)
    below = (section, (inner + n_inner - 1) % n_inner)
    partner = at(1, 0)

    peers = [partner, above, below] + [at(h, d) for h, d in CORES[1:] + RING[1:] + ACROSS[1:2] + ACROSS[3:]]
    barrier = pltpu.get_barrier_semaphore()
    for peer in peers:
        pl.semaphore_signal(barrier, inc=1, device_id=peer, device_id_type=MESH)

    small = [
        pltpu.make_async_copy(source, target, small_load.at[k])
        for k, (source, target) in enumerate(
            ((dims_hbm, dims_ref), (wave_hbm, wave_ref), (mpo_hbm, mpo_ref), (charge_hbm, charge_ref))
        )
    ]
    small[0].start()
    small[1].start()

    def env_rows(k, factor):
        first, last = CHUNKS[k]
        return pl.ds(first * PAIRS * factor, (last - first) * PAIRS * factor)

    loads = [
        pltpu.make_async_copy(env_ref.at[env_rows(k, 2)], env_buf.at[env_rows(k, 2)], env_load.at[k])
        for k in range(len(CHUNKS))
    ]
    for load in loads + small[2:]:
        load.start()

    row8 = lax.broadcasted_iota(jnp.int32, (8, 128), 0)
    lane8 = lax.broadcasted_iota(jnp.int32, (8, 128), 1)

    def partial(x, y):
        prod = x * y
        tiles = [
            prod[8 * i : 8 * i + 8, 128 * j : 128 * j + 128] for i in range(BLK // 8) for j in range(WIDTH // 128)
        ]
        while len(tiles) > 1:
            tiles = [tiles[2 * n] + tiles[2 * n + 1] for n in range(len(tiles) // 2)]
        tile = tiles[0] + pltpu.roll(tiles[0], 64, 1)
        return tile + pltpu.roll(tile, 32, 1)

    def packed(tiles):
        total = jnp.zeros((8, 128), F32)
        for k, tile in enumerate(tiles):
            total = jnp.where(lane8 // 32 == k, tile, total)
        return jnp.sum(total, axis=0, keepdims=True)

    def dots(pairs):
        return packed([partial(x, y) for x, y in pairs])

    def send_row(buf, group, value, send, recv):
        buf[0:1, :] = value
        for h, d in sorted(group[1:], key=distance, reverse=True):
            j = group.index((h, d))
            pltpu.make_async_remote_copy(
                src_ref=buf.at[pl.ds(0, 1)],
                dst_ref=buf.at[pl.ds(j, 1)],
                send_sem=send,
                recv_sem=recv,
                device_id=at(h, d),
                device_id_type=MESH,
            ).start()

    def await_rows(buf, group, sem):
        rows = buf.at[pl.ds(1, len(group) - 1)]
        pltpu.make_async_copy(rows, rows, sem).wait()

    def total_rows(tile):
        for step in (4, 2, 1):
            tile = tile + pltpu.roll(tile, step, 0)
        return tile

    def scalars(tile):
        return jnp.sum(jnp.where(lane8 // 32 == row8, tile, 0.0), axis=1, keepdims=True) * (1.0 / entries)

    def sum_start(k, row):
        send_row(exchange.at[k], EVERY, row, red_send.at[k], red_recv.at[k])

    def sum_finish(k):
        await_rows(exchange.at[k], EVERY, red_recv.at[k])
        part = [exchange[k, 8 * n : 8 * n + 8, :] for n in range(4)]
        return scalars(total_rows((part[0] + part[1]) + (part[2] + part[3])))

    def halo_copies(k):
        return [
            pltpu.make_async_remote_copy(
                src_ref=halo.at[k, 1],
                dst_ref=halo.at[k, 2 * side],
                send_sem=halo_send.at[k, side],
                recv_sem=halo_recv.at[k, side],
                device_id=target,
                device_id_type=MESH,
            )
            for side, target in ((0, above), (1, below))
        ]

    def channels(first, last, midway=None, size=GROUP):
        groups = [(a, min(a + size, last)) for a in range(first, last, size)]

        def left(group):
            a, b = group
            out = jnp.dot(lsel[a * BLK : b * BLK, :], sources[...], preferred_element_type=F32).astype(BF16)
            return [to_mixed(out[k * BLK : (k + 1) * BLK]) for k in range(b - a)]

        total = None
        ready = left(groups[0])
        for n, (a, b) in enumerate(groups):
            now = ready
            if n + 1 < len(groups):
                ready = left(groups[n + 1])
            if midway is not None and n == len(groups) // 2:
                midway()
            mixed = [
                jnp.dot(wsel[a + k], now[k], preferred_element_type=F32).astype(BF16) for k in range(b - a)
            ]
            right = rsel[a:b].reshape((b - a) * 256, 256)
            part = jnp.dot(jnp.concatenate(mixed, axis=1), right, preferred_element_type=F32)
            total = part if total is None else total + part
        return total

    def unmix(total):
        low = low_half(16)
        for j in range(PH // 2):
            lanes = slice(128 * j, 128 * j + 128)
            for p in range(2):
                a = total[32 * j : 32 * j + 16, 128 * p : 128 * p + 128]
                b = total[32 * j + 16 : 32 * j + 32, 128 * p : 128 * p + 128]
                for half, value in enumerate(interchange(a, b, low)):
                    rows = slice(32 * p + 16 * half, 32 * p + 16 * half + 16)
                    vec_t[rows, lanes] = value * mask[rows, :]

    small[0].wait()
    small[1].wait()
    row = lax.broadcasted_iota(jnp.int32, (BLK, 128), 0)
    lane = lax.broadcasted_iota(jnp.int32, (BLK, 128), 1)
    live = (row < dims_ref[0, 0]) & (lane % BLK < dims_ref[0, 1])
    mask[...] = jnp.where(live, 1.0, 0.0).astype(F32)
    start = wave_ref[0] * jnp.concatenate([mask[...]] * (WIDTH // 128), axis=1)
    start_buf[...] = start
    halo[0, 1] = start.astype(BF16)
    norm_row = dots([(start, start)])

    for k in range(len(CHUNKS)):
        loads[k].wait()
        wide[env_rows(k, 2), :] = env_buf[env_rows(k, 2), :].astype(F32)
        first, last = CHUNKS[k]
        count = (last - first) * PAIRS
        upper = wide[pl.ds(first * PAIRS * 2, count, stride=2), :]
        lower = wide[pl.ds(first * PAIRS * 2 + 1, count, stride=2), :]
        for side, value in enumerate((jnp.where(even, upper, lower), jnp.where(even, lower, upper))):
            for a in range(last - first):
                here = (first + a) * PAIRS
                x, y = value[a * PAIRS : a * PAIRS + 16], value[a * PAIRS + 16 : (a + 1) * PAIRS]
                evens, odds = interchange(x, y, low_half(16))
                woven[side, pl.ds(here, 16, stride=2), :] = evens
                woven[side, pl.ds(here + 1, 16, stride=2), :] = odds
        raw[parity, env_rows(k, 1), :] = woven[0, env_rows(k, 1), :].astype(BF16)
        outgoing[env_rows(k, 1), :] = woven[1, env_rows(k, 1), :].astype(BF16)

    pl.semaphore_wait(barrier, len(peers))
    env_copies = [
        pltpu.make_async_remote_copy(
            src_ref=outgoing.at[env_rows(k, 1)],
            dst_ref=raw.at[parity, env_rows(k, 1)],
            send_sem=env_send.at[k],
            recv_sem=env_recv.at[k],
            device_id=partner,
            device_id_type=MESH,
        )
        for k in range(len(CHUNKS))
    ]
    start_halo = halo_copies(0)
    env_copies[0].start()
    for copy in start_halo:
        copy.start()
    for copy in env_copies[1:]:
        copy.start()
    send_row(near_buf.at[0], CORES, norm_row, near_send.at[0], near_recv.at[0])

    zero = jnp.zeros((2 * BLK, 128), BF16)
    for a in range(CHAN):
        rsel[a, 0:128, 128:256] = zero
        rsel[a, 128:256, 0:128] = zero

    def four(k):
        part = [near_buf[k, n : n + 1, :] for n in range(4)]
        return (part[0] + part[1]) + (part[2] + part[3])

    await_rows(near_buf.at[0], CORES, near_recv.at[0])
    norm_row = near_buf[0, 0:1, :] + near_buf[0, 1:2, :]
    send_row(near_buf.at[1], RING, norm_row, near_send.at[1], near_recv.at[1])

    def iota(shape, axis):
        return lax.broadcasted_iota(jnp.int32, shape, axis)

    small[2].wait()
    small[3].wait()
    flat = mpo_ref[...].reshape(PH * PH, CHAN)
    unit_rows = (iota((CHAN, CHAN), 0) == iota((CHAN, CHAN), 1)).astype(BF16)
    by_channel = lax.dot_general(unit_rows, flat, (((1,), (1,)), ((), ())), preferred_element_type=F32)
    keep_t = iota((PH, 256), 1) % 16 == iota((PH, 256), 0)
    picked = jnp.concatenate(
        [jnp.where(keep_t, jnp.broadcast_to(by_channel[a : a + 1, :], (PH, 256)), 0.0) for a in range(CHAN)], axis=0
    ).astype(BF16)
    widen = (iota((256, 256), 0) // 16 == iota((256, 256), 1) // 16).astype(BF16)
    terms = jnp.dot(picked, widen, preferred_element_type=F32).astype(BF16)
    spread_rows = (iota((256, PH), 0) // 16 == iota((256, PH), 1)).astype(BF16)
    same = iota((256, 256), 0) % 16 == iota((256, 256), 1) % 16
    for a in range(CHAN):
        both = jnp.dot(spread_rows, terms[a * PH : (a + 1) * PH], preferred_element_type=F32)
        wsel[a] = jnp.where(same, both, 0.0).astype(BF16)

    low32 = low_half(32)
    low64 = low_half(64)

    def doubled(slot, a):
        x = raw[slot, a * PAIRS : (a + 1) * PAIRS, :]
        turned = pltpu.roll(x, BLK, 1)
        return jnp.where(low32, x, turned), jnp.where(low32, turned, x)

    def place_left(first, last):
        for a in range(first, last):
            charge = charge_ref[a]
            here = jnp.where(low32, -1, 0) == charge
            there = jnp.logical_and(low32, charge == 1)
            for half, value in enumerate(doubled(0, a)):
                rows = slice(a * BLK + half * PAIRS, a * BLK + (half + 1) * PAIRS)
                none = jnp.zeros_like(value)
                lsel[rows, 0:128] = jnp.where(here, value, none)
                lsel[rows, 128:192] = jnp.where(there, value, none)[:, :BLK]

    def place_right(first, last):
        none = jnp.zeros((BLK, 128), BF16)
        for a in range(first, last):
            both = jnp.concatenate(doubled(1, a), axis=0)
            block = jnp.concatenate([jnp.where(low64, both, none), jnp.where(low64, none, both)], axis=0)
            rsel[a, 0:128, 0:128] = block
            rsel[a, 128:256, 128:256] = block

    @pl.when(even)
    def _():
        place_left(0, CHAN)

    @pl.when(jnp.logical_not(even))
    def _():
        place_right(0, CHAN)

    await_rows(near_buf.at[1], RING, near_recv.at[1])
    send_row(near_buf.at[2], ACROSS, four(1), near_send.at[2], near_recv.at[2])

    def receive(k):
        first, last = CHUNKS[k]
        arrived = raw.at[1 - parity, env_rows(k, 1)]
        pltpu.make_async_copy(arrived, arrived, env_recv.at[k]).wait()

        @pl.when(even)
        def _():
            place_right(first, last)

        @pl.when(jnp.logical_not(even))
        def _():
            place_left(first, last)

    receive(0)
    for copy in start_halo:
        copy.wait_recv()
    for k in range(3):
        sources[k * BLK : (k + 1) * BLK, :] = halo[0, k]
    for k, (first, last) in enumerate(CHUNKS):
        if k:
            receive(k)
        if k:
            image[...] += channels(first, last)
        else:
            image[...] = channels(first, last)

    await_rows(near_buf.at[2], ACROSS, near_recv.at[2])
    norm_row = four(2)
    norm = jnp.sum(jnp.where(lane8[0:1] < 32, norm_row, 0.0), axis=1, keepdims=True) * (1.0 / entries)
    scale = 1.0 / jnp.sqrt(norm + EPSILON)
    unmix(image[...])
    im = vec_t[...] * scale
    vec_im[...] = im
    halo[1, 1] = im.astype(BF16)
    halos = [halo_copies(1), halo_copies(2)]
    for copy in halos[0]:
        copy.start()
    psi = start_buf[...] * scale
    start_buf[...] = psi

    def scalar(total, k):
        return total[k : k + 1, :]

    def rotation(energy, coupling, curvature):
        x = 0.5 * (curvature - energy)
        size = jnp.maximum(jnp.abs(x), jnp.abs(coupling))
        safe = jnp.where(size > 0.0, size, 1.0)
        xs, ys = x / safe, -coupling / safe
        radius = jnp.sqrt(xs * xs + ys * ys)
        radius = jnp.where(size > 0.0, radius, 1.0)
        cos2 = jnp.where(size > 0.0, xs / radius, 1.0)
        sin2 = ys / radius
        big = jnp.sqrt(0.5 + 0.5 * jnp.abs(cos2))
        small = 0.5 * sin2 / big
        sign = jnp.where(coupling < 0.0, 1.0, -1.0)
        cosine = jnp.where(cos2 >= 0.0, big, jnp.abs(small))
        sine = jnp.where(cos2 >= 0.0, small, sign * big)
        lowest = 0.5 * (energy + curvature) - jnp.sqrt(x * x + coupling * coupling)
        return cosine, sine, lowest

    def kappa_of(unit, square):
        return unit / jnp.sqrt(unit * unit * square + EPSILON)

    def own(row):
        return scalars(jnp.broadcast_to(row, (8, 128)))

    share = 1.0 / (2 * n_inner)
    row_sums = dots([(psi, im), (im, im), (psi, psi)])
    sum_start(0, row_sums)
    local = own(row_sums)
    weight = jnp.maximum(scalar(local, 2), 0.5 * share)
    quotient = scalar(local, 0) / weight
    sources[BLK : 2 * BLK, :] = (vec_im[...] - quotient * start_buf[...]).astype(BF16)
    scaled = quotient * scale
    for copy in halos[0]:
        copy.wait_recv()
    for k in (0, 2):
        field = halo[1, k].astype(F32) - scaled * halo[0, k].astype(F32)
        sources[k * BLK : (k + 1) * BLK, :] = field.astype(BF16)
    found = {}

    def read_first():
        totals = sum_finish(0)
        energy = scalar(totals, 0)
        square = scalar(totals, 1)
        unit = jnp.sqrt(square + EPSILON)
        inverse = 1.0 / unit
        im = vec_im[...]
        q = (im - energy * start_buf[...]) * inverse
        vec_q[...] = q
        im_buf[...] = ((quotient - energy) * inverse) * im
        rest = square + energy * (energy * scalar(totals, 2) - 2.0 * energy)
        floor = 0.5 * share * jnp.maximum(rest * inverse * inverse, 1e-6)
        found[0] = energy, unit, inverse, floor, partial(q, q), partial(q, im)

    unmix(channels(0, CHAN, read_first, 5))
    energy_now, unit, inverse, floor, part_qq, part_qi = found[0]
    t = vec_t[...] * inverse + im_buf[...]
    vec_t[...] = t
    halo[2, 1] = t.astype(BF16)
    for copy in halos[1]:
        copy.start()

    t = vec_t[...]
    row_sums = packed([part_qq, part_qi, partial(vec_q[...], t), partial(start_buf[...], t)])
    sum_start(1, row_sums)
    local = own(row_sums)
    along_q = scalar(local, 2) / jnp.maximum(scalar(local, 0), floor)
    along_psi = scalar(local, 3) / weight
    sources[BLK : 2 * BLK, :] = (vec_t[...] - along_q * vec_q[...] - along_psi * start_buf[...]).astype(BF16)
    of_im = along_q * inverse
    of_start = (along_psi - of_im * energy_now) * scale
    for copy in halos[1]:
        copy.wait_recv()
    for k in (0, 2):
        field = halo[2, k].astype(F32) - of_im * halo[1, k].astype(F32) - of_start * halo[0, k].astype(F32)
        sources[k * BLK : (k + 1) * BLK, :] = field.astype(BF16)

    def read_second():
        totals = sum_finish(1)
        kappa = kappa_of(unit, scalar(totals, 0))
        coupling = kappa * scalar(totals, 1)
        curvature = kappa * kappa * scalar(totals, 2)
        mirrored = kappa * scalar(totals, 3)
        cosine, sine, _ = rotation(energy_now, coupling, curvature)
        energy = (
            cosine * cosine * energy_now + cosine * sine * (coupling + mirrored) + sine * sine * curvature
        )
        turn = sine * kappa
        im_then, t_then = vec_im[...], vec_t[...]
        psi = cosine * start_buf[...] + turn * vec_q[...]
        im = cosine * im_then + turn * t_then
        q = (im - energy * psi) * inverse
        known = (cosine * unit + turn * along_q) * t_then + (cosine * energy_now + turn * along_psi) * im_then
        start_buf[...] = psi
        vec_q[...] = q
        vec_im[...] = (known - energy * im) * inverse
        found[1] = energy, turn * inverse, partial(q, q), partial(q, im)

    unmix(channels(0, CHAN, read_second, 5))
    energy_next, factor, part_qq, part_qi = found[1]
    t = vec_t[...] * factor + vec_im[...]
    sum_start(2, packed([part_qq, part_qi, partial(vec_q[...], t)]))
    totals = sum_finish(2)
    kappa = kappa_of(unit, scalar(totals, 0))
    coupling = kappa * scalar(totals, 1)
    curvature = kappa * kappa * scalar(totals, 2)
    cosine, sine, lowest = rotation(energy_next, coupling, curvature)
    psi_ref[0] = cosine * start_buf[...] + (sine * kappa) * vec_q[...]
    energy_ref[...] = jnp.broadcast_to(lowest, (1, 128))

    for k, group in enumerate((CORES, RING, ACROSS)):
        await_rows(near_buf.at[k], group, near_send.at[k])
    for k in range(3):
        await_rows(exchange.at[k], EVERY, red_send.at[k])
    for copies in [env_copies, start_halo] + halos:
        for copy in copies:
            copy.wait_send()


def body(wavefunction, environments, mpo_terms, sector_dims, channel_charges):
    rows = environments.reshape(2, CHAN, PAIRS, 128).transpose(1, 2, 0, 3).reshape(CHAN * PAIRS * 2, 128)
    terms = mpo_terms.transpose(1, 2, 0)
    vmem = pl.BlockSpec(memory_space=pltpu.VMEM)
    hbm = pl.BlockSpec(memory_space=pltpu.HBM)
    psi, energy = pl.pallas_call(
        kernel,
        out_shape=(
            pltpu.VMEM((1, BLK, WIDTH), F32),
            pltpu.VMEM((1, 128), F32),
        ),
        in_specs=[hbm] * 5,
        out_specs=(vmem, vmem),
        scratch_shapes=[
            pltpu.VMEM((1, BLK, WIDTH), F32),
            pltpu.VMEM((PH, PH, CHAN), BF16),
            pltpu.SMEM((1, 2), jnp.int32),
            pltpu.SMEM((CHAN,), jnp.int32),
            pltpu.VMEM((2 * CHAN * PAIRS, 128), BF16),
            pltpu.VMEM((2 * CHAN * PAIRS, 128), F32),
            pltpu.VMEM((2, CHAN * PAIRS, 128), F32),
            pltpu.VMEM((2, CHAN * PAIRS, 128), BF16),
            pltpu.VMEM((CHAN * PAIRS, 128), BF16),
            pltpu.VMEM((CHAN * BLK, 3 * BLK), BF16),
            pltpu.VMEM((CHAN, 256, 256), BF16),
            pltpu.VMEM((CHAN, 256, 256), BF16),
            pltpu.VMEM((256, 256), F32),
            pltpu.VMEM((3 * BLK, WIDTH), BF16),
            pltpu.VMEM((3, 3, BLK, WIDTH), BF16),
            pltpu.VMEM((BLK, 128), F32),
            pltpu.VMEM((BLK, WIDTH), F32),
            pltpu.VMEM((BLK, WIDTH), F32),
            pltpu.VMEM((BLK, WIDTH), F32),
            pltpu.VMEM((BLK, WIDTH), F32),
            pltpu.VMEM((BLK, WIDTH), F32),
            pltpu.VMEM((3, 8, 128), F32),
            pltpu.VMEM((3, 32, 128), F32),
            pltpu.SemaphoreType.DMA((4,)),
            pltpu.SemaphoreType.DMA((len(CHUNKS),)),
            pltpu.SemaphoreType.DMA((len(CHUNKS),)),
            pltpu.SemaphoreType.DMA((len(CHUNKS),)),
            pltpu.SemaphoreType.DMA((3, 2)),
            pltpu.SemaphoreType.DMA((3, 2)),
            pltpu.SemaphoreType.DMA((3,)),
            pltpu.SemaphoreType.DMA((3,)),
            pltpu.SemaphoreType.DMA((3,)),
            pltpu.SemaphoreType.DMA((3,)),
        ],
        compiler_params=pltpu.CompilerParams(
            collective_id=0, has_side_effects=True, vmem_limit_bytes=56 * 2**20
        ),
    )(wavefunction, rows, terms, sector_dims, channel_charges)
    return psi, energy[0, :1]


def solution(mesh):
    return jax.shard_map(
        body,
        mesh=mesh,
        in_specs=(
            P(("section", "inner"), None, None),
            P(("section", "inner"), None, None),
            P(),
            P(("section", "inner"), None),
            P(),
        ),
        out_specs=(P(("section", "inner"), None, None), P("section")),
        check_vma=False,
    )
```
